512 devices in a mesh: geo: 16 (over z, core), freq: 32 (over y, x).
Axes of the slice: x: 4, y: 8, z: 8, core: 2. Of those that a mesh axis runs over, the one named last changes fastest.
Arguments:
- adjoint_final: bfloat16 [32, 36, 64, 2048], P('freq', None, None, 'geo'), may hold values from 0.099609375 to 1
- trajectory: bfloat16 [2, 1152, 131072], P(None, None, ('geo', 'freq')), may hold values from 0.099609375 to 2
- interaction: bfloat16 [1152, 1152], replicated, may hold values from -0.1875 to 0.1875
- friction_factor: float32 [32, 131072], P(None, ('geo', 'freq')), may hold values from 0.2 to 1.6
- friction_coeff: float32 [64], replicated, may hold values from 0.25 to 2
- courant_lon: float32 [32, 36], replicated, may hold values from -0.45 to 0.45
- courant_lat: float32 [32, 36], replicated, may hold values from -0.45 to 0.45
- sea_mask: int32 [64, 2048], P(None, 'geo'), may hold values 0 or 1
- sediment: int32 [131072], P(('geo', 'freq')), may hold values from 0 to 63, as said below
Outputs:
- adjoint_initial: bfloat16 [1152, 131072], P(None, ('geo', 'freq'))
- sensitivity: float32 [64], replicated
The draws below stay inside these ranges and needn't reach their ends.
Inputs may be any that keep to these rules, and one draw needn't show every extreme that they name: `sediment`: every group 0 .. 63 occurs.
All inputs are finite; a program needn't handle non-finite values. No bound on the sum of `sea_mask` on one device may be relied on, other than what follows from the above.
Results may differ from the reference program's by a relative error of at most 0.0057.
Values may be sent and summed in bfloat16 or wider, within the bound.
No kernel may reach another device: no remote copies, remote signals or barrier semaphores. Data moves between devices by JAX's collectives and lax.ppermute only.
A program may use at most 64 MiB of HBM per device.

```python
import math
import jax
import jax.numpy as jnp
from jax import lax

ND = 36
NF = 32
K = 1152
NG = 64
LON_DEV = 128
STEPS = 2
SUBSTEPS = 2
PTS_DEV = 256
NLAT = 64
NLON = 2048
NPTS = 131072
N_GEO = 16


def draw_sediment(key, part):
    base = jnp.arange(NPTS, dtype=jnp.int32) * NG // NPTS
    jitter = jax.random.randint(key, (NPTS,), -1, 2, dtype=jnp.int32)
    return jnp.clip(base + jitter, 0, NG - 1).astype(jnp.int32)


def set_ends(entries, key, least, high):
    extent = entries.shape
    index_at = [jax.random.randint(jax.random.fold_in(key, axis), (), 0, extent[axis]) for axis in range(len(extent))]
    entries = entries.at[tuple(index_at)].set(least)
    longest = extent.index(max(extent))
    index_at[longest] = (index_at[longest] + 1) % extent[longest]
    return entries.at[tuple(index_at)].set(high)


def block_levels(own_key, shape, pieces, smallest, high):
    factor_of = 1.0
    for dim, shards_of in pieces:
        steps = jax.random.uniform(jax.random.fold_in(jax.random.fold_in(own_key, 6), dim), (shards_of,), jnp.float32, smallest / len(pieces), high / len(pieces))
        factor_of = factor_of * jnp.repeat(jnp.exp(steps), shape[dim] // shards_of).reshape((-1,) + (1,) * (len(shape) - 1 - dim))
    return factor_of


def gaussian(rng, dims, width, reach, kind=jnp.bfloat16):
    array = jax.random.normal(rng, dims, jnp.float32) * width
    return jnp.minimum(jnp.maximum(array, -reach), reach).astype(kind)


def setup_inputs(seed: int = 0) -> dict:
    key_of = jax.random.split(jax.random.key(seed), 10)
    return {
        "adjoint_final": jnp.clip(jnp.exp(math.log(1.0) - 2.306499 * jax.random.uniform(key_of[0], (NF, ND, NLAT, NLON), jnp.float32) ** block_levels(key_of[0], (NF, ND, NLAT, NLON), ((0, 32), (3, 16)), -0.2, 0.2)), 0.099609375, 1.0).astype(jnp.bfloat16),
        "trajectory": jnp.clip(jnp.exp(math.log(2.0) - 2.9996462 * jax.random.uniform(key_of[1], (STEPS, K, NPTS), jnp.float32) ** block_levels(key_of[1], (STEPS, K, NPTS), ((2, 512),), -0.2, 0.2)), 0.099609375, 2.0).astype(jnp.bfloat16),
        "interaction": gaussian(key_of[2], (K, K), K ** -0.5, 0.1875),
        "friction_factor": jnp.clip(jnp.exp(math.log(1.6) - 2.0794415 * jax.random.uniform(key_of[3], (NF, NPTS), jnp.float32) ** block_levels(key_of[3], (NF, NPTS), ((1, 512),), -0.2, 0.2)), 0.2, 1.6),
        "friction_coeff": jnp.clip(jnp.exp(jax.random.uniform(key_of[4], (NG,), jnp.float32, math.log(0.25), math.log(2.0))), 0.25, 2.0),
        "courant_lon": jnp.clip(jax.random.uniform(key_of[5], (NF, ND), jnp.float32, -0.45, 0.45), -0.45, 0.45),
        "courant_lat": jnp.clip(jax.random.uniform(key_of[6], (NF, ND), jnp.float32, -0.45, 0.45), -0.45, 0.45),
        "sea_mask": set_ends((jax.random.randint(key_of[7], (NLAT, NLON), 0, 4) < 3).astype(jnp.int32), jax.random.fold_in(key_of[7], 1), 0, 1),
        "sediment": draw_sediment(jax.random.fold_in(key_of[9], 71), 0),
    }


step_weight = 0.25


def into_points(field):
    return field.reshape(NF, ND, NLAT, N_GEO, LON_DEV).transpose(0, 1, 3, 2, 4).reshape(K, NPTS)


def into_grid(values):
    return values.reshape(NF, ND, N_GEO, NLAT, LON_DEV).transpose(0, 1, 3, 2, 4).reshape(NF, ND, NLAT, NLON)


def propagate_adjoint(field, courant_lon, courant_lat):
    def one_freq(packed):
        plane, lon_rate, lat_rate = packed
        east_side = jnp.roll(plane, -1, axis=2)
        west_side = jnp.roll(plane, 1, axis=2)
        zero_row = jnp.zeros_like(plane[:, :1, :])
        north_row = jnp.concatenate([plane[:, 1:, :], zero_row], axis=1)
        south_row = jnp.concatenate([zero_row, plane[:, :-1, :]], axis=1)
        lon_abs = jnp.abs(lon_rate)[:, None, None]
        lat_abs = jnp.abs(lat_rate)[:, None, None]
        lon_term = jnp.where((lon_rate > 0)[:, None, None], east_side, west_side)
        lat_term = jnp.where((lat_rate > 0)[:, None, None], north_row, south_row)
        result = (1.0 - lon_abs - lat_abs) * plane + lon_abs * lon_term + lat_abs * lat_term
        return result.astype(jnp.bfloat16)
    return lax.map(one_freq, (field, courant_lon, courant_lat))


def source_adjoint(adjoint, start_state, kappa_rows, coeff_point, interaction):
    freq_count = kappa_rows.shape[0]
    components, columns = adjoint.shape
    factor = jnp.broadcast_to(kappa_rows[:, None, :], (freq_count, components // freq_count, columns)).reshape(components, columns)
    friction = factor * coeff_point[None, :]
    states = [start_state]
    for substep in range(SUBSTEPS - 1):
        current = states[-1]
        squares = (current * current).astype(jnp.bfloat16)
        forced = jnp.dot(interaction, squares, preferred_element_type=jnp.float32)
        states.append(current + step_weight * (forced - friction * current))
    weights = jnp.zeros((columns,), jnp.float32)
    for substep in range(SUBSTEPS - 1, -1, -1):
        current = states[substep]
        weights = weights + jnp.sum(adjoint * factor * current, axis=0)
        pulled = lax.dot_general(interaction, adjoint.astype(jnp.bfloat16), (((0,), (0,)), ((), ())), preferred_element_type=jnp.float32)
        adjoint = adjoint + step_weight * (2.0 * current * pulled - friction * adjoint)
    return adjoint, weights


def reference(adjoint_final, trajectory, interaction, friction_factor, friction_coeff, courant_lon, courant_lat, sea_mask, sediment):
    mask = sea_mask.astype(jnp.bfloat16)
    coeff_all = friction_coeff[sediment]
    blocks = NPTS // PTS_DEV

    def blocked(values):
        return values.reshape(values.shape[0], blocks, PTS_DEV).transpose(1, 0, 2)

    coeff_blocks = coeff_all.reshape(blocks, PTS_DEV)
    total = jnp.zeros((NG,), jnp.float32)
    grid_now = adjoint_final
    new_points = None
    for step_index in range(STEPS - 1, -1, -1):
        field = (grid_now * mask).astype(jnp.float32)
        moved = into_points(propagate_adjoint(field, courant_lon, courant_lat)).astype(jnp.float32)

        def one_block(packed):
            return source_adjoint(packed[0], packed[1].astype(jnp.float32), packed[2], packed[3], interaction)

        adjoint_blocks, weight_blocks = lax.map(one_block, (blocked(moved), blocked(trajectory[step_index]), blocked(friction_factor), coeff_blocks))
        new_points = adjoint_blocks.transpose(1, 0, 2).reshape(K, NPTS).astype(jnp.bfloat16)
        weights = weight_blocks.reshape(NPTS)
        total = total + jax.ops.segment_sum(weights, sediment, num_segments=NG)
        grid_now = into_grid(new_points)
    sensitivity = total * (-step_weight * NG / (NPTS * K))
    return new_points, sensitivity
```

```python
import functools

import jax
import jax.numpy as jnp
from jax import lax
from jax.experimental import pallas as pl
from jax.experimental.pallas import tpu as pltpu
from jax.sharding import PartitionSpec as P

F32 = jnp.float32
BF16 = jnp.bfloat16
step_weight = 0.25
PAD = 40
MIB = 1 << 20
WHOLE = pl.BlockSpec(memory_space=pltpu.VMEM)


def call(kernel, outs, args, scratch=(), flops=0, limit=32):
    size = sum(a.size * a.dtype.itemsize for a in (*args, *outs))
    return pl.pallas_call(
        kernel,
        out_shape=outs,
        in_specs=[WHOLE] * len(args),
        out_specs=[WHOLE] * len(outs),
        scratch_shapes=list(scratch),
        compiler_params=pltpu.CompilerParams(vmem_limit_bytes=limit * MIB),
        cost_estimate=pl.CostEstimate(flops=flops, bytes_accessed=size, transcendentals=0),
    )(*args)


def shape(dims, kind):
    return jax.ShapeDtypeStruct(dims, kind)


def edge_picks(width, lon):
    row = lax.broadcasted_iota(jnp.int32, (16, width), 0)
    lane = lax.broadcasted_iota(jnp.int32, (16, width), 1)
    picks = jnp.zeros((16, width), F32)
    for half in range(width // lon):
        picks = jnp.where((row == half) & (lane == half * lon), 1.0, picks)
        picks = jnp.where((row == 8 + half) & (lane == half * lon + lon - 1), 1.0, picks)
    return picks.astype(BF16)


def take_edges(values, picks):
    return lax.dot_general(picks, values, (((1,), (1,)), ((), ())), preferred_element_type=F32)


def put_edges(from_west, from_east, width, lon):
    both = jnp.concatenate([from_west.astype(F32), from_east.astype(F32)], axis=0).astype(BF16)
    return lax.dot_general(
        both, edge_picks(width, lon), (((0,), (0,)), ((), ())), preferred_element_type=F32
    )


def split_rates(lon_rate, lat_rate):
    lon_abs, lat_abs = jnp.abs(lon_rate), jnp.abs(lat_rate)
    east = jnp.where(lon_rate > 0, lon_abs, 0.0)
    north = jnp.where(lat_rate > 0, lat_abs, 0.0)
    return 1.0 - lon_abs - lat_abs, east, lon_abs - east, north, lat_abs - north


def regroup_kernel(field_ref, mask_ref, rows_ref, west_ref, east_ref):
    directions, lat, lon = field_ref.shape
    rows = directions * lat
    mask = mask_ref[...].astype(F32)
    rows_ref[0:PAD, :] = jnp.zeros((PAD, lon), F32)
    rows_ref[PAD + rows :, :] = jnp.zeros((PAD, lon), F32)
    for d in range(directions):
        rows_ref[pl.ds(PAD + d, lat, stride=directions), :] = field_ref[d].astype(F32) * mask
    edges = take_edges(rows_ref[PAD : PAD + rows, :].astype(BF16), edge_picks(lon, lon))
    west_ref[...] = edges[0:8].astype(BF16)
    east_ref[...] = edges[8:16].astype(BF16)


def interior_kernel(rows_ref, lon_ref, lat_ref, part_ref, rate_ref, lon_scr, lat_scr):
    freqs, directions = lon_ref.shape
    peers, height, lon = part_ref.shape
    own = lax.broadcasted_iota(jnp.int32, (freqs, lon), 0) == lax.axis_index("freq")
    own = own.astype(F32)
    for ref, scr in ((lon_ref, lon_scr), (lat_ref, lat_scr)):
        rate = lax.dot_general(
            ref[...], own, (((0,), (0,)), ((), ())),
            precision=lax.Precision.HIGHEST, preferred_element_type=F32,
        )
        for at in range(0, height, directions):
            scr[at : at + directions, :] = rate
    center, east, west, north, south = split_rates(lon_scr[...], lat_scr[...])
    lane = lax.broadcasted_iota(jnp.int32, (height, lon), 1)
    rate_ref[...] = jnp.where(lane == 0, west, east)
    east = jnp.where(lane == lon - 1, 0.0, east)
    west = jnp.where(lane == 0, 0.0, west)
    for r in range(peers):
        at = PAD + r * height
        here = rows_ref[at : at + height, :]
        part_ref[r] = (
            center * here
            + east * pltpu.roll(here, lon - 1, 1)
            + west * pltpu.roll(here, 1, 1)
            + north * rows_ref[at + directions : at + directions + height, :]
            + south * rows_ref[at - directions : at - directions + height, :]
        )


def edges_kernel(part_ref, rate_ref, west_ref, east_ref, out_ref):
    peers, height, lon = part_ref.shape
    cols = put_edges(west_ref[...], east_ref[...], lon, lon)
    rate = rate_ref[...]
    for r in range(peers):
        out_ref[r] = (part_ref[r] + rate * cols[r * height : (r + 1) * height]).astype(BF16)


def rates_kernel(lon_ref, lat_ref, center_ref, east_ref, west_ref, north_ref, south_ref, scr):
    freqs, directions = lon_ref.shape
    lanes = center_ref.shape[1]
    turned = []
    for ref in (lon_ref, lat_ref):
        scr[...] = jnp.zeros_like(scr)
        scr[0:freqs, 0:directions] = ref[...]
        turned.append(scr[...].T)
    refs = (center_ref, east_ref, west_ref, north_ref, south_ref)
    for f in range(freqs):
        cols = [jnp.broadcast_to(t[0:directions, f : f + 1], (directions, lanes)) for t in turned]
        for ref, rate in zip(refs, split_rates(*cols)):
            ref[f * directions : (f + 1) * directions, :] = rate


def group_hits(sediment, groups):
    points = sediment.shape[1]
    return (lax.broadcasted_iota(jnp.int32, (groups, points), 0) == sediment).astype(F32)


def states_kernel(
    traj_ref, inter_ref, kappa_ref, coeff_ref, sed_ref, turned_ref, decay_ref, factor_ref, next_ref
):
    steps, components, points = traj_ref.shape
    freqs = kappa_ref.shape[0]
    directions = components // freqs
    groups = coeff_ref.shape[1]
    hits = group_hits(sed_ref[...], groups)
    coeff = jnp.dot(
        jnp.broadcast_to(coeff_ref[...], (8, groups)), hits,
        precision=lax.Precision.HIGHEST, preferred_element_type=F32,
    )[0:1]
    for f in range(freqs):
        factor_ref[f * directions : (f + 1) * directions, :] = jnp.broadcast_to(
            kappa_ref[f : f + 1, :], (directions, points)
        )
    decay_ref[...] = 1.0 - step_weight * (factor_ref[...] * coeff)
    turned_ref[...] = inter_ref[...].T
    chunk = components // 4
    for n in range(steps):
        state = traj_ref[n]
        squares = state * state
        for at in range(0, components, chunk):
            forced = jnp.dot(inter_ref[at : at + chunk, :], squares, preferred_element_type=F32)
            here = traj_ref[n, at : at + chunk, :].astype(F32)
            next_ref[n, at : at + chunk, :] = (
                decay_ref[at : at + chunk, :] * here + step_weight * forced
            )


def two_substeps(m_scr, r_scr, turned_ref, decay_ref, factor_ref, next_ref, traj_ref, n, write):
    components, points = m_scr.shape
    chunk = components // 4
    weights = jnp.zeros((8, points), F32)
    moved = r_scr[...]
    for at in range(0, components, chunk):
        rows = slice(at, at + chunk)
        pulled = jnp.dot(turned_ref[rows, :], moved, preferred_element_type=F32)
        after, state = next_ref[n, rows, :], traj_ref[n, rows, :].astype(F32)
        old = m_scr[rows, :]
        new = decay_ref[rows, :] * old + 0.5 * (after * pulled)
        terms = factor_ref[rows, :] * (old * after + new * state)
        weights = weights + terms.reshape(chunk // 8, 8, points).sum(axis=0)
        m_scr[rows, :] = new
        r_scr[rows, :] = new.astype(BF16)
    moved = r_scr[...]
    for at in range(0, components, chunk):
        rows = slice(at, at + chunk)
        pulled = jnp.dot(turned_ref[rows, :], moved, preferred_element_type=F32)
        state = traj_ref[n, rows, :].astype(F32)
        write(rows, decay_ref[rows, :] * m_scr[rows, :] + 0.5 * (state * pulled))
    return weights


def first_kernel(
    n, moved_ref, turned_ref, decay_ref, factor_ref, next_ref, traj_ref, mask_ref,
    low_ref, high_ref, west_ref, east_ref, weights_ref, m_scr, r_scr,
):
    freqs, height, lon = moved_ref.shape
    directions = height // 2
    for f in range(freqs):
        block = moved_ref[f].astype(F32)
        rows = slice(f * directions, (f + 1) * directions)
        m_scr[rows, 0:lon] = block[0:directions]
        m_scr[rows, lon : 2 * lon] = block[directions:height]
    r_scr[...] = m_scr[...].astype(BF16)
    mask = mask_ref[...]
    picks = edge_picks(2 * lon, lon)

    def write(rows, values):
        masked = (values * mask).astype(BF16)
        low_ref[rows, :] = masked[:, 0:lon]
        high_ref[rows, :] = masked[:, lon : 2 * lon]
        r_scr[rows, :] = masked

    weights_ref[...] = two_substeps(
        m_scr, r_scr, turned_ref, decay_ref, factor_ref, next_ref, traj_ref, n, write
    )
    edges = take_edges(r_scr[...], picks)
    west_ref[...] = edges[0:8].astype(BF16)
    east_ref[...] = edges[8:16].astype(BF16)


def second_kernel(
    n, low_ref, high_ref, north_ref, south_ref, west_ref, east_ref,
    center_rate, east_rate, west_rate, north_rate, south_rate,
    turned_ref, decay_ref, factor_ref, next_ref, traj_ref, sed_ref, weights_ref,
    out_ref, sums_ref, m_scr, r_scr,
):
    components, lon = low_ref.shape
    cols = put_edges(west_ref[...], east_ref[...], 2 * lon, lon)
    chunk = components // 8
    lane = lax.broadcasted_iota(jnp.int32, (chunk, lon), 1)
    for at in range(0, components, chunk):
        rows = slice(at, at + chunk)
        low, high = low_ref[rows, :].astype(F32), high_ref[rows, :].astype(F32)
        above, below = north_ref[rows, :].astype(F32), south_ref[rows, :].astype(F32)
        for half, (here, up, down) in enumerate(((low, high, below), (high, above, low))):
            lanes = slice(half * lon, (half + 1) * lon)
            edge = cols[rows, lanes]
            east = jnp.where(lane == lon - 1, edge, pltpu.roll(here, lon - 1, 1))
            west = jnp.where(lane == 0, edge, pltpu.roll(here, 1, 1))
            value = (
                center_rate[rows, :] * here
                + east_rate[rows, :] * east
                + west_rate[rows, :] * west
                + north_rate[rows, :] * up
                + south_rate[rows, :] * down
            ).astype(BF16)
            r_scr[rows, lanes] = value
            m_scr[rows, lanes] = value.astype(F32)

    def write(rows, values):
        out_ref[rows, :] = values.astype(BF16)

    weights = weights_ref[...] + two_substeps(
        m_scr, r_scr, turned_ref, decay_ref, factor_ref, next_ref, traj_ref, n, write
    )
    hits = group_hits(sed_ref[...], sums_ref.shape[2])
    sums = lax.dot_general(
        weights, hits, (((1,), (1,)), ((), ())),
        precision=lax.Precision.HIGHEST, preferred_element_type=F32,
    )
    sums_ref[...] = jnp.broadcast_to(sums[None], sums_ref.shape)


def add_kernel(parts_ref, out_ref):
    out_ref[...] = jnp.broadcast_to(parts_ref[...].sum(axis=0)[None], out_ref.shape)


def final_kernel(scale, parts_ref, out_ref):
    total = parts_ref[...].sum(axis=0).sum(axis=0, keepdims=True)
    out_ref[...] = total[:, 0 : out_ref.shape[1]] * scale


def shards(
    adjoint_final, trajectory, interaction, friction_factor, friction_coeff,
    courant_lon, courant_lat, sea_mask, sediment,
):
    freq_local, directions, lat, lon = adjoint_final.shape
    steps, components, points = trajectory.shape
    groups = friction_coeff.shape[0]
    peers, regions = lax.axis_size("freq"), lax.axis_size("geo")
    me = lax.axis_index("freq")
    rows = directions * lat
    height = rows // peers
    eastward = [(i, (i + 1) % regions) for i in range(regions)]
    westward = [(j, i) for i, j in eastward]
    northward = [(i, i + 1) for i in range(peers - 1)]
    southward = [(j, i) for i, j in northward]

    field = adjoint_final.reshape(directions, lat, lon)
    grouped, west, east = call(
        regroup_kernel,
        [shape((rows + 2 * PAD, lon), F32), shape((8, rows), BF16), shape((8, rows), BF16)],
        [field, sea_mask],
    )
    from_west = lax.ppermute(east, "geo", eastward)
    from_east = lax.ppermute(west, "geo", westward)
    part, rate = call(
        interior_kernel,
        [shape((peers, height, lon), F32), shape((height, lon), F32)],
        [grouped, courant_lon, courant_lat],
        [pltpu.VMEM((height, lon), F32), pltpu.VMEM((height, lon), F32)],
    )
    (sent,) = call(
        edges_kernel, [shape((peers, height, lon), BF16)], [part, rate, from_west, from_east]
    )
    sent, trajectory, courant_lon, courant_lat = lax.optimization_barrier(
        (sent, trajectory, courant_lon, courant_lat)
    )
    moved = lax.all_to_all(sent, "freq", split_axis=0, concat_axis=0, tiled=True)

    sediment_row = sediment.reshape(1, points)
    mask_row = lax.dynamic_slice_in_dim(sea_mask, me * (points // lon), points // lon, 0)
    mask_row = mask_row.astype(F32).reshape(1, points)
    turned, decay, factor, following = call(
        states_kernel,
        [
            shape((components, components), BF16),
            shape((components, points), F32),
            shape((components, points), F32),
            shape((steps, components, points), F32),
        ],
        [trajectory, interaction, friction_factor, friction_coeff.reshape(1, groups), sediment_row],
        flops=4 * components * components * points,
    )
    rates = call(
        rates_kernel,
        [shape((components, lon), F32)] * 5,
        [courant_lon, courant_lat],
        [pltpu.VMEM((128, 128), F32)],
    )
    carried = [pltpu.VMEM((components, points), F32), pltpu.VMEM((components, points), BF16)]
    low, high, west, east, weights = call(
        functools.partial(first_kernel, 1),
        [
            shape((components, lon), BF16),
            shape((components, lon), BF16),
            shape((8, components), BF16),
            shape((8, components), BF16),
            shape((8, points), F32),
        ],
        [moved, turned, decay, factor, following, trajectory, mask_row],
        carried,
        flops=4 * components * components * points,
    )
    above = lax.ppermute(low, "freq", southward)
    below = lax.ppermute(high, "freq", northward)
    from_west = lax.ppermute(east, "geo", eastward)
    from_east = lax.ppermute(west, "geo", westward)
    result, sums = call(
        functools.partial(second_kernel, 0),
        [shape((components, points), BF16), shape((peers, 8, 128), F32)],
        [
            low, high, above, below, from_west, from_east, *rates,
            turned, decay, factor, following, trajectory, sediment_row, weights,
        ],
        carried,
        flops=4 * components * components * points,
    )
    sums = lax.all_to_all(sums, "freq", split_axis=0, concat_axis=0, tiled=True)
    (sums,) = call(add_kernel, [shape((regions, 8, 128), F32)], [sums])
    sums = lax.all_to_all(sums, "geo", split_axis=0, concat_axis=0, tiled=True)
    point_total = points * peers * regions
    scale = -step_weight * groups / (point_total * components)
    (total,) = call(functools.partial(final_kernel, scale), [shape((1, groups), F32)], [sums])
    return result, total.reshape(groups)


def solution(mesh):
    in_specs = (
        P("freq", None, None, "geo"),
        P(None, None, ("geo", "freq")),
        P(),
        P(None, ("geo", "freq")),
        P(),
        P(),
        P(),
        P(None, "geo"),
        P(("geo", "freq")),
    )
    out_specs = (P(None, ("geo", "freq")), P())
    return jax.shard_map(shards, mesh=mesh, in_specs=in_specs, out_specs=out_specs, check_vma=False)
```

```python
import functools

import jax
import jax.numpy as jnp
from jax import lax
from jax.experimental import pallas as pl
from jax.experimental.pallas import tpu as pltpu
from jax.sharding import PartitionSpec as P

F32 = jnp.float32
BF16 = jnp.bfloat16
step_weight = 0.25
PAD = 40
MIB = 1 << 20
WHOLE = pl.BlockSpec(memory_space=pltpu.VMEM)
OUTSIDE = pl.BlockSpec(memory_space=pl.ANY)


def call(kernel, outs, args, scratch=(), flops=0, late=None, limit=32):
    late = {} if late is None else late
    places = sorted(late)
    size = sum(a.size * a.dtype.itemsize for a in (*args, *outs))
    args = [
        pltpu.with_memory_space_constraint(a, pltpu.HBM) if i in late else a
        for i, a in enumerate(args)
    ]
    n = len(args) + len(outs) + len(scratch)

    def body(*refs):
        given, kept, buffers = list(refs[: len(args)]), refs[len(args) : n], refs[n:]
        copies = {}
        for k, i in enumerate(places):
            source = given[i] if late[i] is None else given[i].at[late[i]]
            copies[i] = pltpu.make_async_copy(source, buffers[k], buffers[-1].at[k])
            copies[i].start()
            given[i] = buffers[k]
        if places:
            kernel(*given, *kept, wait=lambda *which: [copies[i].wait() for i in which])
        else:
            kernel(*given, *kept)

    buffers = [
        pltpu.VMEM(args[i].shape if late[i] is None else args[i].shape[1:], args[i].dtype)
        for i in places
    ]
    if places:
        buffers.append(pltpu.SemaphoreType.DMA((len(places),)))
    return pl.pallas_call(
        body,
        out_shape=outs,
        in_specs=[OUTSIDE if i in late else WHOLE for i in range(len(args))],
        out_specs=[WHOLE] * len(outs),
        scratch_shapes=[*scratch, *buffers],
        compiler_params=pltpu.CompilerParams(vmem_limit_bytes=limit * MIB),
        cost_estimate=pl.CostEstimate(flops=flops, bytes_accessed=size, transcendentals=0),
    )(*args)


def shape(dims, kind):
    return jax.ShapeDtypeStruct(dims, kind)


def edge_picks(width, lon):
    row = lax.broadcasted_iota(jnp.int32, (16, width), 0)
    lane = lax.broadcasted_iota(jnp.int32, (16, width), 1)
    picks = jnp.zeros((16, width), F32)
    for half in range(width // lon):
        picks = jnp.where((row == half) & (lane == half * lon), 1.0, picks)
        picks = jnp.where((row == 8 + half) & (lane == half * lon + lon - 1), 1.0, picks)
    return picks.astype(BF16)


def take_edges(values, picks):
    return lax.dot_general(picks, values, (((1,), (1,)), ((), ())), preferred_element_type=F32)


def put_edges(from_west, from_east, width, lon):
    both = jnp.concatenate([from_west.astype(F32), from_east.astype(F32)], axis=0).astype(BF16)
    return lax.dot_general(
        both, edge_picks(width, lon), (((0,), (0,)), ((), ())), preferred_element_type=F32
    )


def split_rates(lon_rate, lat_rate):
    lon_abs, lat_abs = jnp.abs(lon_rate), jnp.abs(lat_rate)
    east = jnp.where(lon_rate > 0, lon_abs, 0.0)
    north = jnp.where(lat_rate > 0, lat_abs, 0.0)
    return 1.0 - lon_abs - lat_abs, east, lon_abs - east, north, lat_abs - north


def regroup_kernel(
    field_ref, mask_ref, lon_ref, lat_ref, rows_ref, west_ref, east_ref, rates_ref, wait
):
    directions, lat, lon = field_ref.shape
    freqs = lon_ref.shape[0]
    rows = directions * lat
    height = rates_ref.shape[1]
    rows_ref[0:PAD, :] = jnp.zeros((PAD, lon), F32)
    rows_ref[PAD + rows :, :] = jnp.zeros((PAD, lon), F32)
    own = lax.broadcasted_iota(jnp.int32, (freqs, lon), 0) == lax.axis_index("freq")
    own = own.astype(F32)
    wait(2, 3)
    for at in range(0, height, directions):
        for slot, ref in enumerate((lon_ref, lat_ref)):
            rates_ref[slot, at : at + directions, :] = lax.dot_general(
                ref[...], own, (((0,), (0,)), ((), ())),
                precision=lax.Precision.HIGHEST, preferred_element_type=F32,
            )
    wait(0, 1)
    mask = mask_ref[...].astype(F32)
    for d in range(directions):
        rows_ref[pl.ds(PAD + d, lat, stride=directions), :] = field_ref[d].astype(F32) * mask
    edges = take_edges(rows_ref[PAD : PAD + rows, :].astype(BF16), edge_picks(lon, lon))
    west_ref[...] = edges[0:8].astype(BF16)
    east_ref[...] = edges[8:16].astype(BF16)


def interior_kernel(rows_ref, rates_ref, part_ref, rate_ref, *, directions):
    peers, height, lon = part_ref.shape
    center, east, west, north, south = split_rates(rates_ref[0], rates_ref[1])
    lane = lax.broadcasted_iota(jnp.int32, (height, lon), 1)
    rate_ref[...] = jnp.where(lane == 0, west, east)
    east = jnp.where(lane == lon - 1, 0.0, east)
    west = jnp.where(lane == 0, 0.0, west)
    for r in range(peers):
        at = PAD + r * height
        here = rows_ref[at : at + height, :]
        part_ref[r] = (
            center * here
            + east * pltpu.roll(here, lon - 1, 1)
            + west * pltpu.roll(here, 1, 1)
            + north * rows_ref[at + directions : at + directions + height, :]
            + south * rows_ref[at - directions : at - directions + height, :]
        )


def edges_kernel(part_ref, rate_ref, west_ref, east_ref, out_ref):
    peers, height, lon = part_ref.shape
    cols = put_edges(west_ref[...], east_ref[...], lon, lon)
    rate = rate_ref[...]
    for r in range(peers):
        out_ref[r] = (part_ref[r] + rate * cols[r * height : (r + 1) * height]).astype(BF16)


def spread_rates(courant_refs, turn_scr, rates_scr):
    freqs, directions = courant_refs[0].shape
    for slot, ref in enumerate(courant_refs):
        turn_scr[...] = jnp.zeros_like(turn_scr)
        turn_scr[0:freqs, 0:directions] = ref[...]
        turned = turn_scr[...].T
        for f in range(freqs):
            rates_scr[slot, f * directions : (f + 1) * directions, :] = jnp.broadcast_to(
                turned[0:directions, f : f + 1], (directions, rates_scr.shape[2])
            )


def spread_factor(kappa_ref, factor_scr):
    freqs, points = kappa_ref.shape
    directions = factor_scr.shape[0] // freqs
    for f in range(freqs):
        factor_scr[f * directions : (f + 1) * directions, :] = jnp.broadcast_to(
            kappa_ref[f : f + 1, :], (directions, points)
        )


def decay_of(factor, coeff):
    return 1.0 - step_weight * (factor * coeff)


def states_kernel(
    traj_ref, inter_ref, kappa_ref, coeff_ref, sed_ref,
    turned_ref, point_coeff_ref, next1_ref, next0_ref, low_ref, high_ref, west_ref, east_ref,
    factor_scr, product_scr, pull_scr, wait,
):
    steps, components, points = traj_ref.shape
    groups = coeff_ref.shape[1]
    lon = low_ref.shape[1]
    wait(2, 3, 4)
    sediment = sed_ref[...]
    hits = (lax.broadcasted_iota(jnp.int32, (groups, points), 0) == sediment).astype(F32)
    coeff = jnp.dot(
        jnp.broadcast_to(coeff_ref[...], (8, groups)), hits,
        precision=lax.Precision.HIGHEST, preferred_element_type=F32,
    )[0:1]
    point_coeff_ref[...] = coeff
    spread_factor(kappa_ref, factor_scr)
    wait(0, 1)
    turned_ref[...] = inter_ref[...].T
    chunk = components // 4
    for n, next_ref in ((0, next0_ref), (1, next1_ref)):
        state = traj_ref[n]
        squares = state * state
        for at in range(0, components, chunk):
            rows = slice(at, at + chunk)
            forced = jnp.dot(inter_ref[rows, :], squares, preferred_element_type=F32)
            here = traj_ref[n, rows, :].astype(F32)
            factor = factor_scr[rows, :]
            after = decay_of(factor, coeff) * here + step_weight * forced
            next_ref[rows, :] = after
            if n == 0:
                product_scr[rows, :] = (0.5 * factor * here * after).astype(BF16)
    product = product_scr[...]
    for at in range(0, components, chunk):
        rows = slice(at, at + chunk)
        pushed = jnp.dot(inter_ref[rows, :], product, preferred_element_type=F32)
        factor, here = factor_scr[rows, :], traj_ref[0, rows, :].astype(F32)
        pull = factor * (next0_ref[rows, :] + decay_of(factor, coeff) * here) + pushed
        pull_scr[rows, :] = pull.astype(BF16)
    extra = pull_scr.shape[0] - components
    first_row = lax.broadcasted_iota(jnp.int32, (extra, points), 0) == 0
    pull_scr[components:, :] = jnp.where(first_row, sediment.astype(F32), 0.0).astype(BF16)
    low_ref[...] = pull_scr[:, 0:lon]
    high_ref[...] = pull_scr[:, lon : 2 * lon]
    edges = take_edges(pull_scr[...], edge_picks(2 * lon, lon))
    west_ref[...] = edges[0:8].astype(BF16)
    east_ref[...] = edges[8:16].astype(BF16)


def fields_kernel(
    low_ref, high_ref, above_ref, below_ref, west_ref, east_ref, courant_lon_ref, courant_lat_ref,
    fields_ref, near_ref, turn_scr, rates_scr, wait,
):
    total, lon = low_ref.shape
    components = rates_scr.shape[1]
    cols = put_edges(west_ref[...], east_ref[...], 2 * lon, lon)
    wait(6, 7)
    spread_rates((courant_lon_ref, courant_lat_ref), turn_scr, rates_scr)
    near_ref[...] = jnp.zeros_like(near_ref)
    chunk = components // 8
    for at, size in [(i, chunk) for i in range(0, components, chunk)] + [(components, total - components)]:
        rows = slice(at, at + size)
        lane = lax.broadcasted_iota(jnp.int32, (size, lon), 1)
        low, high = low_ref[rows, :].astype(F32), high_ref[rows, :].astype(F32)
        above, below = above_ref[rows, :].astype(F32), below_ref[rows, :].astype(F32)
        if at < components:
            rates = split_rates(rates_scr[0, rows, :], rates_scr[1, rows, :])
        for half, (here, up, down) in enumerate(((low, high, below), (high, above, low))):
            lanes = slice(half * lon, (half + 1) * lon)
            edge = cols[rows, lanes]
            west = jnp.where(lane == 0, edge, pltpu.roll(here, 1, 1))
            east = jnp.where(lane == lon - 1, edge, pltpu.roll(here, lon - 1, 1))
            for slot, value in enumerate((here, west, east, down, up)):
                if at < components:
                    fields_ref[slot, rows, lanes] = (rates[slot] * value).astype(BF16)
                else:
                    near_ref[slot : slot + 1, lanes] = value[0:1]


def two_substeps(m_scr, r_scr, turned_ref, factor_scr, coeff, ready, write, weigh):
    components, points = m_scr.shape
    chunk = components // 4
    weights = jnp.zeros((8, points), F32)
    moved = r_scr[...]
    for at in range(0, components, chunk):
        rows = slice(at, at + chunk)
        pulled = jnp.dot(turned_ref[rows, :], moved, preferred_element_type=F32)
        after, state = ready(rows)
        factor, old = factor_scr[rows, :], m_scr[rows, :]
        new = decay_of(factor, coeff) * old + 0.5 * (after * pulled)
        if weigh:
            terms = factor * (old * after + new * state)
            weights = weights + terms.reshape(chunk // 8, 8, points).sum(axis=0)
        m_scr[rows, :] = new
        r_scr[rows, :] = new.astype(BF16)
    moved = r_scr[...]
    for at in range(0, components, chunk):
        rows = slice(at, at + chunk)
        pulled = jnp.dot(turned_ref[rows, :], moved, preferred_element_type=F32)
        state = ready(rows)[1]
        new = decay_of(factor_scr[rows, :], coeff) * m_scr[rows, :] + 0.5 * (state * pulled)
        write(rows, new)
    return weights


def first_kernel(
    moved_ref, turned_ref, kappa_ref, coeff_ref, mask_ref, near_ref, next_ref, traj_ref, fields_ref,
    low_ref, high_ref, west_ref, east_ref, sums_ref, m_scr, r_scr, factor_scr, wait,
):
    freqs, height, lon = moved_ref.shape
    points = 2 * lon
    directions = height // 2
    for f in range(freqs):
        block = moved_ref[f].astype(F32)
        rows = slice(f * directions, (f + 1) * directions)
        m_scr[rows, 0:lon] = block[0:directions]
        m_scr[rows, lon:points] = block[directions:height]
    r_scr[...] = m_scr[...].astype(BF16)
    wait(2)
    spread_factor(kappa_ref, factor_scr)
    wait(3, 4, 5, 6, 7, 8)
    mask = mask_ref[pl.ds(2 * lax.axis_index("freq"), 2), :].astype(F32)
    picks = edge_picks(points, lon)
    slots = fields_ref.shape[0]
    weights = [jnp.zeros((8, points), F32)] * slots

    def ready(rows):
        return next_ref[rows, :], traj_ref[rows, :].astype(F32)

    def write(rows, values):
        low = (values[:, 0:lon] * mask[0:1]).astype(BF16)
        high = (values[:, lon:points] * mask[1:2]).astype(BF16)
        low_ref[rows, :] = low
        high_ref[rows, :] = high
        next_ref[rows, 0:lon] = low.astype(F32)
        next_ref[rows, lon:points] = high.astype(F32)

    own = two_substeps(m_scr, r_scr, turned_ref, factor_scr, coeff_ref[...], ready, write, True)
    components = m_scr.shape[0]
    edges = take_edges(next_ref[...].astype(BF16), picks)
    west_ref[...] = edges[0:8].astype(BF16)
    east_ref[...] = edges[8:16].astype(BF16)
    chunk = components // 4
    for at in range(0, components, chunk):
        rows = slice(at, at + chunk)
        value = next_ref[rows, :]
        for slot in range(slots):
            terms = fields_ref[slot, rows, :].astype(F32) * value
            weights[slot] = weights[slot] + terms.reshape(chunk // 8, 8, points).sum(axis=0)
    weights[0] = weights[0] + own
    sums = jnp.zeros(sums_ref.shape[1:], F32)
    group = lax.broadcasted_iota(jnp.int32, (sums.shape[1], points), 0).astype(F32)
    for slot in range(slots):
        hits = (group == near_ref[slot : slot + 1, :]).astype(F32)
        sums = sums + lax.dot_general(
            weights[slot], hits, (((1,), (1,)), ((), ())),
            precision=lax.Precision.HIGHEST, preferred_element_type=F32,
        )
    sums_ref[...] = jnp.broadcast_to(sums[None], sums_ref.shape)


def second_kernel(
    low_ref, high_ref, north_ref, south_ref, west_ref, east_ref,
    turned_ref, kappa_ref, coeff_ref, next_ref, traj_ref, courant_lon_ref, courant_lat_ref,
    out_ref, m_scr, r_scr, factor_scr, turn_scr, rates_scr, wait,
):
    components, lon = low_ref.shape
    wait(11, 12)
    spread_rates((courant_lon_ref, courant_lat_ref), turn_scr, rates_scr)
    wait(7)
    spread_factor(kappa_ref, factor_scr)
    cols = put_edges(west_ref[...], east_ref[...], 2 * lon, lon)
    chunk = components // 8
    lane = lax.broadcasted_iota(jnp.int32, (chunk, lon), 1)
    for at in range(0, components, chunk):
        rows = slice(at, at + chunk)
        low, high = low_ref[rows, :].astype(F32), high_ref[rows, :].astype(F32)
        above, below = north_ref[rows, :].astype(F32), south_ref[rows, :].astype(F32)
        rates = split_rates(rates_scr[0, rows, :], rates_scr[1, rows, :])
        for half, (here, up, down) in enumerate(((low, high, below), (high, above, low))):
            lanes = slice(half * lon, (half + 1) * lon)
            edge = cols[rows, lanes]
            east = jnp.where(lane == lon - 1, edge, pltpu.roll(here, lon - 1, 1))
            west = jnp.where(lane == 0, edge, pltpu.roll(here, 1, 1))
            value = (
                rates[0] * here
                + rates[1] * east
                + rates[2] * west
                + rates[3] * up
                + rates[4] * down
            ).astype(BF16)
            r_scr[rows, lanes] = value
            m_scr[rows, lanes] = value.astype(F32)

    wait(8, 9, 10)

    def ready(rows):
        return next_ref[rows, :], traj_ref[rows, :].astype(F32)

    def write(rows, values):
        out_ref[rows, :] = values.astype(BF16)

    two_substeps(m_scr, r_scr, turned_ref, factor_scr, coeff_ref[...], ready, write, False)


def add_kernel(parts_ref, out_ref):
    out_ref[...] = jnp.broadcast_to(parts_ref[...].sum(axis=0)[None], out_ref.shape)


def final_kernel(scale, parts_ref, out_ref):
    total = parts_ref[...].sum(axis=0).sum(axis=0, keepdims=True)
    out_ref[...] = total[:, 0 : out_ref.shape[1]] * scale


def shards(
    adjoint_final, trajectory, interaction, friction_factor, friction_coeff,
    courant_lon, courant_lat, sea_mask, sediment,
):
    freq_local, directions, lat, lon = adjoint_final.shape
    steps, components, points = trajectory.shape
    groups = friction_coeff.shape[0]
    peers, regions = lax.axis_size("freq"), lax.axis_size("geo")
    rows = directions * lat
    height = rows // peers
    eastward = [(i, (i + 1) % regions) for i in range(regions)]
    westward = [(j, i) for i, j in eastward]
    northward = [(i, i + 1) for i in range(peers - 1)]
    southward = [(j, i) for i, j in northward]

    def swap(low, high, west, east):
        return (
            lax.ppermute(low, "freq", southward),
            lax.ppermute(high, "freq", northward),
            lax.ppermute(east, "geo", eastward),
            lax.ppermute(west, "geo", westward),
        )

    field = adjoint_final.reshape(directions, lat, lon)
    grouped, west, east, own_rates = call(
        regroup_kernel,
        [
            shape((rows + 2 * PAD, lon), F32),
            shape((8, rows), BF16),
            shape((8, rows), BF16),
            shape((2, height, lon), F32),
        ],
        [field, sea_mask, courant_lon, courant_lat],
        late={0: None, 1: None, 2: None, 3: None},
    )
    from_west = lax.ppermute(east, "geo", eastward)
    from_east = lax.ppermute(west, "geo", westward)
    part, rate = call(
        functools.partial(interior_kernel, directions=directions),
        [shape((peers, height, lon), F32), shape((height, lon), F32)],
        [grouped, own_rates],
    )
    (sent,) = call(
        edges_kernel, [shape((peers, height, lon), BF16)], [part, rate, from_west, from_east]
    )
    sent, trajectory, courant_lon, courant_lat = lax.optimization_barrier(
        (sent, trajectory, courant_lon, courant_lat)
    )
    moved = lax.all_to_all(sent, "freq", split_axis=0, concat_axis=0, tiled=True)

    product = 2 * components * components * points
    full, half_full = (components, points), (components, lon)
    tall = components + 16
    turned, coeff, next1, next0, *pulls = call(
        states_kernel,
        [
            shape((components, components), BF16),
            shape((1, points), F32),
            shape(full, F32),
            shape(full, F32),
            shape((tall, lon), BF16),
            shape((tall, lon), BF16),
            shape((8, tall), BF16),
            shape((8, tall), BF16),
        ],
        [
            trajectory, interaction, friction_factor, friction_coeff.reshape(1, groups),
            sediment.reshape(1, points),
        ],
        [pltpu.VMEM(full, F32), pltpu.VMEM(full, BF16), pltpu.VMEM((tall, points), BF16)],
        flops=3 * product,
        late={0: None, 1: None, 2: None, 3: None, 4: None},
    )

    spread = [pltpu.VMEM((128, 128), F32), pltpu.VMEM((2, *half_full), F32)]
    fields, near = call(
        fields_kernel,
        [shape((5, *full), BF16), shape((8, points), F32)],
        [pulls[0], pulls[1], *swap(*pulls), courant_lon, courant_lat],
        spread,
        late={6: None, 7: None},
    )
    carried = [pltpu.VMEM(full, F32), pltpu.VMEM(full, BF16), pltpu.VMEM(full, F32)]
    low, high, west, east, sums = call(
        first_kernel,
        [
            shape(half_full, BF16),
            shape(half_full, BF16),
            shape((8, components), BF16),
            shape((8, components), BF16),
            shape((peers, 8, 128), F32),
        ],
        [moved, turned, friction_factor, coeff, sea_mask, near, next1, trajectory, fields],
        carried,
        flops=2 * product,
        late={2: None, 3: None, 4: None, 5: None, 6: None, 7: 1, 8: None},
    )
    (result,) = call(
        second_kernel,
        [shape(full, BF16)],
        [
            low, high, *swap(low, high, west, east),
            turned, friction_factor, coeff, next0, trajectory, courant_lon, courant_lat,
        ],
        carried + spread,
        flops=2 * product,
        late={7: None, 8: None, 9: None, 10: 0, 11: None, 12: None},
    )
    sums = lax.all_to_all(sums, "freq", split_axis=0, concat_axis=0, tiled=True)
    (sums,) = call(add_kernel, [shape((regions, 8, 128), F32)], [sums])
    sums = lax.all_to_all(sums, "geo", split_axis=0, concat_axis=0, tiled=True)
    point_total = points * peers * regions
    scale = -step_weight * groups / (point_total * components)
    (total,) = call(functools.partial(final_kernel, scale), [shape((1, groups), F32)], [sums])
    return result, total.reshape(groups)


def solution(mesh):
    in_specs = (
        P("freq", None, None, "geo"),
        P(None, None, ("geo", "freq")),
        P(),
        P(None, ("geo", "freq")),
        P(),
        P(),
        P(),
        P(None, "geo"),
        P(("geo", "freq")),
    )
    out_specs = (P(None, ("geo", "freq")), P())
    return jax.shard_map(shards, mesh=mesh, in_specs=in_specs, out_specs=out_specs, check_vma=False)
```

```python
import functools
import math

import jax
import jax.numpy as jnp
from jax import lax
from jax.experimental import pallas as pl
from jax.experimental.pallas import tpu as pltpu
from jax.sharding import PartitionSpec as P

F32 = jnp.float32
BF16 = jnp.bfloat16
step_weight = 0.25
PAD = 40
MIB = 1 << 20
WHOLE = pl.BlockSpec(memory_space=pltpu.VMEM)
OUTSIDE = pl.BlockSpec(memory_space=pl.ANY)


def call(kernel, outs, args, scratch=(), flops=0, late=None, outside=(), limit=32):
    late = {} if late is None else late
    places = sorted(late)
    size = sum(a.size * a.dtype.itemsize for a in (*args, *outs))
    args = [
        pltpu.with_memory_space_constraint(a, pltpu.HBM) if i in late else a
        for i, a in enumerate(args)
    ]
    n = len(args) + len(outs) + len(scratch)

    def body(*refs):
        given, kept, buffers = list(refs[: len(args)]), refs[len(args) : n], refs[n:]
        copies = {}
        for k, i in enumerate(places):
            source = given[i] if late[i] is None else given[i].at[late[i]]
            copies[i] = pltpu.make_async_copy(source, buffers[k], buffers[-1].at[k])
            given[i] = buffers[k]
        for i in sorted(places, key=lambda i: math.prod(given[i].shape)):
            copies[i].start()
        if places:
            kernel(*given, *kept, wait=lambda *which: [copies[i].wait() for i in which])
        else:
            kernel(*given, *kept)

    buffers = [
        pltpu.VMEM(args[i].shape if late[i] is None else args[i].shape[1:], args[i].dtype)
        for i in places
    ]
    if places:
        buffers.append(pltpu.SemaphoreType.DMA((len(places),)))
    return pl.pallas_call(
        body,
        out_shape=outs,
        in_specs=[OUTSIDE if i in late or i in outside else WHOLE for i in range(len(args))],
        out_specs=[WHOLE] * len(outs),
        scratch_shapes=[*scratch, *buffers],
        compiler_params=pltpu.CompilerParams(vmem_limit_bytes=limit * MIB),
        cost_estimate=pl.CostEstimate(flops=flops, bytes_accessed=size, transcendentals=0),
    )(*args)


def shape(dims, kind):
    return jax.ShapeDtypeStruct(dims, kind)


def edge_picks(width, lon):
    row = lax.broadcasted_iota(jnp.int32, (16, width), 0)
    lane = lax.broadcasted_iota(jnp.int32, (16, width), 1)
    picks = jnp.zeros((16, width), F32)
    for half in range(width // lon):
        picks = jnp.where((row == half) & (lane == half * lon), 1.0, picks)
        picks = jnp.where((row == 8 + half) & (lane == half * lon + lon - 1), 1.0, picks)
    return picks.astype(BF16)


def take_edges(values, picks):
    return lax.dot_general(picks, values, (((1,), (1,)), ((), ())), preferred_element_type=F32)


def put_edges(from_west, from_east, width, lon):
    both = jnp.concatenate([from_west.astype(F32)[8:16], from_east.astype(F32)[0:8]], axis=0)
    return lax.dot_general(
        both.astype(BF16), edge_picks(width, lon), (((0,), (0,)), ((), ())),
        preferred_element_type=F32,
    )


def split_rates(lon_rate, lat_rate):
    lon_abs, lat_abs = jnp.abs(lon_rate), jnp.abs(lat_rate)
    east = jnp.where(lon_rate > 0, lon_abs, 0.0)
    north = jnp.where(lat_rate > 0, lat_abs, 0.0)
    return 1.0 - lon_abs - lat_abs, east, lon_abs - east, north, lat_abs - north


def regroup_kernel(
    field_ref, mask_ref, lon_ref, lat_ref, rows_ref, edge_ref, rates_ref, wait
):
    directions, lat, lon = field_ref.shape
    freqs = lon_ref.shape[0]
    rows = directions * lat
    height = rates_ref.shape[1]
    rows_ref[0:PAD, :] = jnp.zeros((PAD, lon), F32)
    rows_ref[PAD + rows :, :] = jnp.zeros((PAD, lon), F32)
    own = lax.broadcasted_iota(jnp.int32, (freqs, lon), 0) == lax.axis_index("freq")
    own = own.astype(F32)
    wait(2, 3)
    for at in range(0, height, directions):
        for slot, ref in enumerate((lon_ref, lat_ref)):
            rates_ref[slot, at : at + directions, :] = lax.dot_general(
                ref[...], own, (((0,), (0,)), ((), ())),
                precision=lax.Precision.HIGHEST, preferred_element_type=F32,
            )
    wait(0, 1)
    mask = mask_ref[...].astype(F32)
    for d in range(directions):
        rows_ref[pl.ds(PAD + d, lat, stride=directions), :] = field_ref[d].astype(F32) * mask
    edges = take_edges(rows_ref[PAD : PAD + rows, :].astype(BF16), edge_picks(lon, lon))
    edge_ref[...] = edges.astype(BF16)


def interior_kernel(rows_ref, rates_ref, part_ref, rate_ref, *, directions):
    peers, height, lon = part_ref.shape
    center, east, west, north, south = split_rates(rates_ref[0], rates_ref[1])
    lane = lax.broadcasted_iota(jnp.int32, (height, lon), 1)
    rate_ref[...] = jnp.where(lane == 0, west, east)
    east = jnp.where(lane == lon - 1, 0.0, east)
    west = jnp.where(lane == 0, 0.0, west)
    for r in range(peers):
        at = PAD + r * height
        here = rows_ref[at : at + height, :]
        part_ref[r] = (
            center * here
            + east * pltpu.roll(here, lon - 1, 1)
            + west * pltpu.roll(here, 1, 1)
            + north * rows_ref[at + directions : at + directions + height, :]
            + south * rows_ref[at - directions : at - directions + height, :]
        )


def edges_kernel(part_ref, rate_ref, west_ref, east_ref, out_ref):
    peers, height, lon = part_ref.shape
    cols = put_edges(west_ref[...], east_ref[...], lon, lon)
    rate = rate_ref[...]
    for r in range(peers):
        out_ref[r] = (part_ref[r] + rate * cols[r * height : (r + 1) * height]).astype(BF16)


def spread_rates(courant_refs, turn_scr, rates_scr):
    freqs, directions = courant_refs[0].shape
    for slot, ref in enumerate(courant_refs):
        turn_scr[...] = jnp.zeros_like(turn_scr)
        turn_scr[0:freqs, 0:directions] = ref[...]
        turned = turn_scr[...].T
        for f in range(freqs):
            rates_scr[slot, f * directions : (f + 1) * directions, :] = jnp.broadcast_to(
                turned[0:directions, f : f + 1], (directions, rates_scr.shape[2])
            )


def spread_factor(kappa_ref, factor_scr):
    freqs, points = kappa_ref.shape
    directions = factor_scr.shape[0] // freqs
    for f in range(freqs):
        factor_scr[f * directions : (f + 1) * directions, :] = jnp.broadcast_to(
            kappa_ref[f : f + 1, :], (directions, points)
        )


def decay_of(factor, coeff):
    return 1.0 - step_weight * (factor * coeff)


def forward(state_ref, inter_ref, factor_scr, coeff, rows):
    forced = jnp.dot(inter_ref[rows, :], square_of(state_ref), preferred_element_type=F32)
    here = state_ref[rows, :].astype(F32)
    return here, decay_of(factor_scr[rows, :], coeff) * here + step_weight * forced


def square_of(state_ref):
    state = state_ref[...]
    return state * state


def blocks_of(size, count):
    return [slice(at, at + size // count) for at in range(0, size, size // count)]


def pull_kernel(
    traj_ref, inter_any, kappa_ref, coeff_ref, sed_ref,
    point_coeff_ref, next_ref, low_ref, high_ref, edge_ref,
    factor_scr, product_scr, pull_scr, inter_ref, sems, wait,
):
    components, points = traj_ref.shape
    groups = coeff_ref.shape[1]
    lon = low_ref.shape[1]
    blocks = blocks_of(components, 4)
    copies = [
        pltpu.make_async_copy(inter_any.at[rows, :], inter_ref.at[rows, :], sems.at[i])
        for i, rows in enumerate(blocks)
    ]
    for copy in copies:
        copy.start()
    wait(2, 3, 4)
    sediment = sed_ref[...]
    hits = (lax.broadcasted_iota(jnp.int32, (groups, points), 0) == sediment).astype(F32)
    coeff = jnp.dot(
        jnp.broadcast_to(coeff_ref[...], (8, groups)), hits,
        precision=lax.Precision.HIGHEST, preferred_element_type=F32,
    )[0:1]
    point_coeff_ref[...] = coeff
    spread_factor(kappa_ref, factor_scr)
    wait(0)
    for copy, rows in zip(copies, blocks):
        copy.wait()
        here, after = forward(traj_ref, inter_ref, factor_scr, coeff, rows)
        next_ref[rows, :] = after
        product_scr[rows, :] = (0.5 * factor_scr[rows, :] * here * after).astype(BF16)
    product = product_scr[...]
    for rows in blocks:
        pushed = jnp.dot(inter_ref[rows, :], product, preferred_element_type=F32)
        factor, here = factor_scr[rows, :], traj_ref[rows, :].astype(F32)
        pull = factor * (next_ref[rows, :] + decay_of(factor, coeff) * here) + pushed
        pull_scr[rows, :] = pull.astype(BF16)
    extra = pull_scr.shape[0] - components
    first_row = lax.broadcasted_iota(jnp.int32, (extra, points), 0) == 0
    pull_scr[components:, :] = jnp.where(first_row, sediment.astype(F32), 0.0).astype(BF16)
    low_ref[...] = pull_scr[:, 0:lon]
    high_ref[...] = pull_scr[:, lon : 2 * lon]
    edge_ref[...] = take_edges(pull_scr[...], edge_picks(2 * lon, lon)).astype(BF16)


def states_kernel(
    traj_ref, inter_ref, kappa_ref, coeff_ref, turned_ref, next_ref, factor_scr, wait
):
    components = traj_ref.shape[0]
    wait(2, 3)
    spread_factor(kappa_ref, factor_scr)
    wait(0, 1)
    coeff = coeff_ref[...]
    turned_ref[...] = inter_ref[...].T
    for rows in blocks_of(components, 4):
        next_ref[rows, :] = forward(traj_ref, inter_ref, factor_scr, coeff, rows)[1]


def sums_kernel(
    low_ref, high_ref, pull_low_ref, pull_high_ref, above_ref, below_ref, west_ref, east_ref,
    courant_lon_ref, courant_lat_ref, own_ref, sums_ref, turn_scr, rates_scr, wait,
):
    components, lon = low_ref.shape
    total = components + 16
    wait(8, 9)
    spread_rates((courant_lon_ref, courant_lat_ref), turn_scr, rates_scr)
    wait(6, 7)
    cols = put_edges(west_ref[...], east_ref[...], 2 * lon, lon)
    wait(2, 3, 4, 5)
    weights = [[jnp.zeros((8, lon), F32)] * 5 for _ in range(2)]
    weights[0][0], weights[1][0] = own_ref[:, 0:lon], own_ref[:, lon : 2 * lon]
    near = [[None] * 5, [None] * 5]
    for rows in [*blocks_of(components, components // 144), slice(components, total)]:
        size = rows.stop - rows.start
        lane = lax.broadcasted_iota(jnp.int32, (size, lon), 1)
        low, high = pull_low_ref[rows, :].astype(F32), pull_high_ref[rows, :].astype(F32)
        above, below = above_ref[rows, :].astype(F32), below_ref[rows, :].astype(F32)
        if rows.start < components:
            rates = split_rates(rates_scr[0, rows, :], rates_scr[1, rows, :])
        for half, (here, up, down, field) in enumerate(
            ((low, high, below, low_ref), (high, above, low, high_ref))
        ):
            edge = cols[rows, half * lon : (half + 1) * lon]
            west = jnp.where(lane == 0, edge, pltpu.roll(here, 1, 1))
            east = jnp.where(lane == lon - 1, edge, pltpu.roll(here, lon - 1, 1))
            reached = (here, west, east, down, up)
            if rows.start == components:
                near[half] = [value[0:1] for value in reached]
                continue
            masked = field[rows, :].astype(F32)
            for slot, value in enumerate(reached):
                terms = (rates[slot] * value * masked).reshape(size // 8, 8, lon)
                weights[half][slot] = weights[half][slot] + terms.sum(axis=0)
    sums = jnp.zeros(sums_ref.shape[1:], F32)
    group = lax.broadcasted_iota(jnp.int32, (sums.shape[1], lon), 0).astype(F32)
    for half in range(2):
        for slot in range(5):
            hits = (group == near[half][slot]).astype(F32)
            sums = sums + lax.dot_general(
                weights[half][slot], hits, (((1,), (1,)), ((), ())),
                precision=lax.Precision.HIGHEST, preferred_element_type=F32,
            )
    sums_ref[...] = jnp.broadcast_to(sums[None], sums_ref.shape)


def two_substeps(m_scr, r_scr, turned_ref, factor_scr, coeff, ready, write, weigh):
    components, points = m_scr.shape
    chunk = components // 4
    weights = jnp.zeros((8, points), F32)
    moved = r_scr[...]
    for at in range(0, components, chunk):
        rows = slice(at, at + chunk)
        pulled = jnp.dot(turned_ref[rows, :], moved, preferred_element_type=F32)
        after, state = ready(rows)
        factor, old = factor_scr[rows, :], m_scr[rows, :]
        new = decay_of(factor, coeff) * old + 0.5 * (after * pulled)
        if weigh:
            terms = factor * (old * after + new * state)
            weights = weights + terms.reshape(chunk // 8, 8, points).sum(axis=0)
        m_scr[rows, :] = new
        r_scr[rows, :] = new.astype(BF16)
    moved = r_scr[...]
    for at in range(0, components, chunk):
        rows = slice(at, at + chunk)
        pulled = jnp.dot(turned_ref[rows, :], moved, preferred_element_type=F32)
        state = ready(rows)[1]
        new = decay_of(factor_scr[rows, :], coeff) * m_scr[rows, :] + 0.5 * (state * pulled)
        write(rows, new)
    return weights


def first_kernel(
    moved_ref, turned_ref, kappa_ref, coeff_ref, mask_ref, next_ref, traj_ref,
    low_ref, high_ref, edge_ref, weights_ref, m_scr, r_scr, factor_scr, wait,
):
    freqs, height, lon = moved_ref.shape
    points = 2 * lon
    directions = height // 2
    for f in range(freqs):
        block = moved_ref[f].astype(F32)
        rows = slice(f * directions, (f + 1) * directions)
        m_scr[rows, 0:lon] = block[0:directions]
        m_scr[rows, lon:points] = block[directions:height]
    r_scr[...] = m_scr[...].astype(BF16)
    wait(2, 3, 4)
    spread_factor(kappa_ref, factor_scr)
    mask = mask_ref[pl.ds(2 * lax.axis_index("freq"), 2), :].astype(F32)
    wait(5, 6)

    def ready(rows):
        return next_ref[rows, :], traj_ref[rows, :].astype(F32)

    def write(rows, values):
        low = (values[:, 0:lon] * mask[0:1]).astype(BF16)
        high = (values[:, lon:points] * mask[1:2]).astype(BF16)
        low_ref[rows, :] = low
        high_ref[rows, :] = high

    weights_ref[...] = two_substeps(
        m_scr, r_scr, turned_ref, factor_scr, coeff_ref[...], ready, write, True
    )
    picks = edge_picks(points, lon)
    edges = take_edges(low_ref[...], picks[:, 0:lon]) + take_edges(high_ref[...], picks[:, lon:points])
    edge_ref[...] = edges.astype(BF16)


def second_kernel(
    low_ref, high_ref, north_ref, south_ref, west_ref, east_ref,
    turned_ref, kappa_ref, coeff_ref, next_ref, traj_ref, courant_lon_ref, courant_lat_ref,
    out_ref, m_scr, r_scr, factor_scr, turn_scr, rates_scr, wait,
):
    components, lon = low_ref.shape
    wait(11, 12)
    spread_rates((courant_lon_ref, courant_lat_ref), turn_scr, rates_scr)
    wait(7)
    spread_factor(kappa_ref, factor_scr)
    cols = put_edges(west_ref[...], east_ref[...], 2 * lon, lon)
    chunk = components // 8
    lane = lax.broadcasted_iota(jnp.int32, (chunk, lon), 1)
    for at in range(0, components, chunk):
        rows = slice(at, at + chunk)
        low, high = low_ref[rows, :].astype(F32), high_ref[rows, :].astype(F32)
        above, below = north_ref[rows, :].astype(F32), south_ref[rows, :].astype(F32)
        rates = split_rates(rates_scr[0, rows, :], rates_scr[1, rows, :])
        for half, (here, up, down) in enumerate(((low, high, below), (high, above, low))):
            lanes = slice(half * lon, (half + 1) * lon)
            edge = cols[rows, lanes]
            east = jnp.where(lane == lon - 1, edge, pltpu.roll(here, lon - 1, 1))
            west = jnp.where(lane == 0, edge, pltpu.roll(here, 1, 1))
            value = (
                rates[0] * here
                + rates[1] * east
                + rates[2] * west
                + rates[3] * up
                + rates[4] * down
            ).astype(BF16)
            r_scr[rows, lanes] = value
            m_scr[rows, lanes] = value.astype(F32)

    wait(8, 9, 10)

    def ready(rows):
        return next_ref[rows, :], traj_ref[rows, :].astype(F32)

    def write(rows, values):
        out_ref[rows, :] = values.astype(BF16)

    two_substeps(m_scr, r_scr, turned_ref, factor_scr, coeff_ref[...], ready, write, False)


def add_kernel(parts_ref, out_ref):
    out_ref[...] = jnp.broadcast_to(parts_ref[...].sum(axis=0)[None], out_ref.shape)


def final_kernel(scale, parts_ref, out_ref):
    total = parts_ref[...].sum(axis=0).sum(axis=0, keepdims=True)
    out_ref[...] = total[:, 0 : out_ref.shape[1]] * scale


def shards(
    adjoint_final, trajectory, interaction, friction_factor, friction_coeff,
    courant_lon, courant_lat, sea_mask, sediment,
):
    freq_local, directions, lat, lon = adjoint_final.shape
    steps, components, points = trajectory.shape
    groups = friction_coeff.shape[0]
    peers, regions = lax.axis_size("freq"), lax.axis_size("geo")
    rows = directions * lat
    height = rows // peers
    eastward = [(i, (i + 1) % regions) for i in range(regions)]
    westward = [(j, i) for i, j in eastward]
    northward = [(i, i + 1) for i in range(peers - 1)]
    southward = [(j, i) for i, j in northward]

    def swap(low, high, edges):
        return (
            lax.ppermute(low, "freq", southward),
            lax.ppermute(high, "freq", northward),
            lax.ppermute(edges, "geo", eastward),
            lax.ppermute(edges, "geo", westward),
        )

    field = adjoint_final.reshape(directions, lat, lon)
    grouped, edges, own_rates = call(
        regroup_kernel,
        [shape((rows + 2 * PAD, lon), F32), shape((16, rows), BF16), shape((2, height, lon), F32)],
        [field, sea_mask, courant_lon, courant_lat],
        late={0: None, 1: None, 2: None, 3: None},
    )
    from_west = lax.ppermute(edges, "geo", eastward)
    from_east = lax.ppermute(edges, "geo", westward)
    part, rate = call(
        functools.partial(interior_kernel, directions=directions),
        [shape((peers, height, lon), F32), shape((height, lon), F32)],
        [grouped, own_rates],
    )
    (sent,) = call(
        edges_kernel, [shape((peers, height, lon), BF16)], [part, rate, from_west, from_east]
    )
    sent, trajectory = lax.optimization_barrier((sent, trajectory))
    moved = lax.all_to_all(sent, "freq", split_axis=0, concat_axis=0, tiled=True)

    product = 2 * components * components * points
    full, half_full = (components, points), (components, lon)
    tall = components + 16
    coeff, next0, pull_low, pull_high, pull_edges = call(
        pull_kernel,
        [
            shape((1, points), F32),
            shape(full, F32),
            shape((tall, lon), BF16),
            shape((tall, lon), BF16),
            shape((16, tall), BF16),
        ],
        [
            trajectory, pltpu.with_memory_space_constraint(interaction, pltpu.HBM),
            friction_factor, friction_coeff.reshape(1, groups), sediment.reshape(1, points),
        ],
        [
            pltpu.VMEM(full, F32), pltpu.VMEM(full, BF16), pltpu.VMEM((tall, points), BF16),
            pltpu.VMEM((components, components), BF16), pltpu.SemaphoreType.DMA((4,)),
        ],
        flops=2 * product,
        late={0: 0, 2: None, 3: None, 4: None},
        outside=(1,),
    )
    pulls = swap(pull_low, pull_high, pull_edges)
    turned, next1 = call(
        states_kernel,
        [shape((components, components), BF16), shape(full, F32)],
        [trajectory, interaction, friction_factor, coeff],
        [pltpu.VMEM(full, F32)],
        flops=product,
        late={0: 1, 1: None, 2: None, 3: None},
    )
    moved, *pulls = lax.optimization_barrier((moved, *pulls))
    carried = [pltpu.VMEM(full, F32), pltpu.VMEM(full, BF16), pltpu.VMEM(full, F32)]
    spread = [pltpu.VMEM((128, 128), F32), pltpu.VMEM((2, *half_full), F32)]
    low, high, edges, weights = call(
        first_kernel,
        [
            shape(half_full, BF16),
            shape(half_full, BF16),
            shape((16, components), BF16),
            shape((8, points), F32),
        ],
        [moved, turned, friction_factor, coeff, sea_mask, next1, trajectory],
        carried,
        flops=2 * product,
        late={2: None, 3: None, 4: None, 5: None, 6: 1},
    )
    swapped = swap(low, high, edges)
    (sums,) = call(
        sums_kernel,
        [shape((peers, 8, 128), F32)],
        [low, high, pull_low, pull_high, *pulls, courant_lon, courant_lat, weights],
        spread,
        late={i: None for i in range(2, 10)},
    )
    above, below, from_west, from_east = swapped
    sums, from_west, from_east = lax.optimization_barrier((sums, from_west, from_east))
    (result,) = call(
        second_kernel,
        [shape(full, BF16)],
        [
            low, high, above, below, from_west, from_east,
            turned, friction_factor, coeff, next0, trajectory, courant_lon, courant_lat,
        ],
        carried + spread,
        flops=2 * product,
        late={7: None, 8: None, 9: None, 10: 0, 11: None, 12: None},
    )
    sums = lax.all_to_all(sums, "freq", split_axis=0, concat_axis=0, tiled=True)
    result, sums = lax.optimization_barrier((result, sums))
    (sums,) = call(add_kernel, [shape((regions, 8, 128), F32)], [sums])
    sums = lax.all_to_all(sums, "geo", split_axis=0, concat_axis=0, tiled=True)
    point_total = points * peers * regions
    scale = -step_weight * groups / (point_total * components)
    (total,) = call(functools.partial(final_kernel, scale), [shape((1, groups), F32)], [sums])
    return result, total.reshape(groups)


def solution(mesh):
    in_specs = (
        P("freq", None, None, "geo"),
        P(None, None, ("geo", "freq")),
        P(),
        P(None, ("geo", "freq")),
        P(),
        P(),
        P(),
        P(None, "geo"),
        P(("geo", "freq")),
    )
    out_specs = (P(None, ("geo", "freq")), P())
    return jax.shard_map(shards, mesh=mesh, in_specs=in_specs, out_specs=out_specs, check_vma=False)
```

```python
import functools
import math

import jax
import jax.numpy as jnp
from jax import lax
from jax.experimental import pallas as pl
from jax.experimental.pallas import tpu as pltpu
from jax.sharding import PartitionSpec as P

F32 = jnp.float32
BF16 = jnp.bfloat16
step_weight = 0.25
PAD = 40
MIB = 1 << 20
WHOLE = pl.BlockSpec(memory_space=pltpu.VMEM)
OUTSIDE = pl.BlockSpec(memory_space=pl.ANY)


def call(kernel, outs, args, scratch=(), flops=0, late=None, outside=(), limit=32):
    late = {} if late is None else late
    places = sorted(late)
    size = sum(a.size * a.dtype.itemsize for a in (*args, *outs))
    args = [
        pltpu.with_memory_space_constraint(a, pltpu.HBM) if i in late else a
        for i, a in enumerate(args)
    ]
    n = len(args) + len(outs) + len(scratch)

    def body(*refs):
        given, kept, buffers = list(refs[: len(args)]), refs[len(args) : n], refs[n:]
        copies = {}
        for k, i in enumerate(places):
            source = given[i] if late[i] is None else given[i].at[late[i]]
            copies[i] = pltpu.make_async_copy(source, buffers[k], buffers[-1].at[k])
            given[i] = buffers[k]
        for i in sorted(places, key=lambda i: math.prod(given[i].shape)):
            copies[i].start()
        if places:
            kernel(*given, *kept, wait=lambda *which: [copies[i].wait() for i in which])
        else:
            kernel(*given, *kept)

    buffers = [
        pltpu.VMEM(args[i].shape if late[i] is None else args[i].shape[1:], args[i].dtype)
        for i in places
    ]
    if places:
        buffers.append(pltpu.SemaphoreType.DMA((len(places),)))
    return pl.pallas_call(
        body,
        out_shape=outs,
        in_specs=[OUTSIDE if i in late or i in outside else WHOLE for i in range(len(args))],
        out_specs=[WHOLE] * len(outs),
        scratch_shapes=[*scratch, *buffers],
        compiler_params=pltpu.CompilerParams(vmem_limit_bytes=limit * MIB),
        cost_estimate=pl.CostEstimate(flops=flops, bytes_accessed=size, transcendentals=0),
    )(*args)


def shape(dims, kind):
    return jax.ShapeDtypeStruct(dims, kind)


def edge_picks(width, lon):
    row = lax.broadcasted_iota(jnp.int32, (16, width), 0)
    lane = lax.broadcasted_iota(jnp.int32, (16, width), 1)
    picks = jnp.zeros((16, width), F32)
    for half in range(width // lon):
        picks = jnp.where((row == half) & (lane == half * lon), 1.0, picks)
        picks = jnp.where((row == 8 + half) & (lane == half * lon + lon - 1), 1.0, picks)
    return picks.astype(BF16)


def take_edges(values, picks):
    return lax.dot_general(picks, values, (((1,), (1,)), ((), ())), preferred_element_type=F32)


def put_edges(from_west, from_east, width, lon):
    both = jnp.concatenate([from_west.astype(F32)[8:16], from_east.astype(F32)[0:8]], axis=0)
    return lax.dot_general(
        both.astype(BF16), edge_picks(width, lon), (((0,), (0,)), ((), ())),
        preferred_element_type=F32,
    )


def split_rates(lon_rate, lat_rate):
    lon_abs, lat_abs = jnp.abs(lon_rate), jnp.abs(lat_rate)
    east = jnp.where(lon_rate > 0, lon_abs, 0.0)
    north = jnp.where(lat_rate > 0, lat_abs, 0.0)
    return 1.0 - lon_abs - lat_abs, east, lon_abs - east, north, lat_abs - north


def regroup_kernel(
    field_ref, mask_ref, lon_ref, lat_ref, rows_ref, edge_ref, rates_ref, wait
):
    directions, lat, lon = field_ref.shape
    freqs = lon_ref.shape[0]
    rows = directions * lat
    height = rates_ref.shape[1]
    rows_ref[0:PAD, :] = jnp.zeros((PAD, lon), F32)
    rows_ref[PAD + rows :, :] = jnp.zeros((PAD, lon), F32)
    own = lax.broadcasted_iota(jnp.int32, (freqs, lon), 0) == lax.axis_index("freq")
    own = own.astype(F32)
    wait(2, 3)
    for at in range(0, height, directions):
        for slot, ref in enumerate((lon_ref, lat_ref)):
            rates_ref[slot, at : at + directions, :] = lax.dot_general(
                ref[...], own, (((0,), (0,)), ((), ())),
                precision=lax.Precision.HIGHEST, preferred_element_type=F32,
            )
    wait(0, 1)
    mask = mask_ref[...].astype(F32)
    for d in range(directions):
        rows_ref[pl.ds(PAD + d, lat, stride=directions), :] = field_ref[d].astype(F32) * mask
    edges = take_edges(rows_ref[PAD : PAD + rows, :].astype(BF16), edge_picks(lon, lon))
    edge_ref[...] = edges.astype(BF16)


def interior_kernel(rows_ref, rates_ref, part_ref, rate_ref, *, directions):
    peers, height, lon = part_ref.shape
    center, east, west, north, south = split_rates(rates_ref[0], rates_ref[1])
    lane = lax.broadcasted_iota(jnp.int32, (height, lon), 1)
    rate_ref[...] = jnp.where(lane == 0, west, east)
    east = jnp.where(lane == lon - 1, 0.0, east)
    west = jnp.where(lane == 0, 0.0, west)
    for r in range(peers):
        at = PAD + r * height
        here = rows_ref[at : at + height, :]
        part_ref[r] = (
            center * here
            + east * pltpu.roll(here, lon - 1, 1)
            + west * pltpu.roll(here, 1, 1)
            + north * rows_ref[at + directions : at + directions + height, :]
            + south * rows_ref[at - directions : at - directions + height, :]
        )


def edges_kernel(part_ref, rate_ref, west_ref, east_ref, out_ref):
    peers, height, lon = part_ref.shape
    cols = put_edges(west_ref[...], east_ref[...], lon, lon)
    rate = rate_ref[...]
    for r in range(peers):
        out_ref[r] = (part_ref[r] + rate * cols[r * height : (r + 1) * height]).astype(BF16)


def spread_rates(courant_refs, turn_scr, rates_scr):
    freqs, directions = courant_refs[0].shape
    for slot, ref in enumerate(courant_refs):
        turn_scr[...] = jnp.zeros_like(turn_scr)
        turn_scr[0:freqs, 0:directions] = ref[...]
        turned = turn_scr[...].T
        for f in range(freqs):
            rates_scr[slot, f * directions : (f + 1) * directions, :] = jnp.broadcast_to(
                turned[0:directions, f : f + 1], (directions, rates_scr.shape[2])
            )


def spread_factor(kappa_ref, factor_scr):
    freqs, points = kappa_ref.shape
    directions = factor_scr.shape[0] // freqs
    for f in range(freqs):
        factor_scr[f * directions : (f + 1) * directions, :] = jnp.broadcast_to(
            kappa_ref[f : f + 1, :], (directions, points)
        )


def decay_of(factor, coeff):
    return 1.0 - step_weight * (factor * coeff)


def forward(state_ref, inter_ref, factor_scr, coeff, rows):
    forced = jnp.dot(inter_ref[rows, :], square_of(state_ref), preferred_element_type=F32)
    here = state_ref[rows, :].astype(F32)
    return here, decay_of(factor_scr[rows, :], coeff) * here + step_weight * forced


def square_of(state_ref):
    state = state_ref[...]
    return state * state


def blocks_of(size, count):
    return [slice(at, at + size // count) for at in range(0, size, size // count)]


def pull_kernel(
    trajectory_ref, inter_ref, kappa_ref, coeff_ref, sed_ref,
    point_coeff_ref, next_ref, pull_ref, factor_scr, product_scr, wait,
):
    traj_ref = trajectory_ref.at[0]
    components, points = traj_ref.shape
    groups = coeff_ref.shape[1]
    blocks = blocks_of(components, 4)
    wait(2, 3, 4)
    sediment = sed_ref[...]
    hits = (lax.broadcasted_iota(jnp.int32, (groups, points), 0) == sediment).astype(F32)
    coeff = jnp.dot(
        jnp.broadcast_to(coeff_ref[...], (8, groups)), hits,
        precision=lax.Precision.HIGHEST, preferred_element_type=F32,
    )[0:1]
    point_coeff_ref[...] = coeff
    spread_factor(kappa_ref, factor_scr)
    for rows in blocks:
        here, after = forward(traj_ref, inter_ref, factor_scr, coeff, rows)
        next_ref[rows, :] = after
        product_scr[rows, :] = (0.5 * factor_scr[rows, :] * here * after).astype(BF16)
    product = product_scr[...]
    for rows in blocks:
        pushed = jnp.dot(inter_ref[rows, :], product, preferred_element_type=F32)
        factor, here = factor_scr[rows, :], traj_ref[rows, :].astype(F32)
        pull = factor * (next_ref[rows, :] + decay_of(factor, coeff) * here) + pushed
        pull_ref[rows, :] = pull.astype(BF16)


def states_kernel(
    trajectory_ref, inter_ref, kappa_ref, coeff_ref, courant_lon_ref, courant_lat_ref,
    turned_ref, next_ref, rates_ref, factor_scr, turn_scr, wait,
):
    traj_ref = trajectory_ref.at[1]
    components = traj_ref.shape[0]
    wait(2, 4, 5)
    spread_factor(kappa_ref, factor_scr)
    spread_rates((courant_lon_ref, courant_lat_ref), turn_scr, rates_ref)
    coeff = coeff_ref[...]
    turned_ref[...] = inter_ref[...].T
    for rows in blocks_of(components, 4):
        next_ref[rows, :] = forward(traj_ref, inter_ref, factor_scr, coeff, rows)[1]


def two_substeps(m_scr, r_scr, turned_ref, factor_scr, coeff, ready, write, weigh):
    components, points = m_scr.shape
    chunk = components // 4
    weights = jnp.zeros((8, points), F32)
    moved = r_scr[...]
    for at in range(0, components, chunk):
        rows = slice(at, at + chunk)
        pulled = jnp.dot(turned_ref[rows, :], moved, preferred_element_type=F32)
        after, state = ready(rows)
        factor, old = factor_scr[rows, :], m_scr[rows, :]
        new = decay_of(factor, coeff) * old + 0.5 * (after * pulled)
        if weigh:
            terms = factor * (old * after + new * state)
            weights = weights + terms.reshape(chunk // 8, 8, points).sum(axis=0)
        m_scr[rows, :] = new
        r_scr[rows, :] = new.astype(BF16)
    moved = r_scr[...]
    for at in range(0, components, chunk):
        rows = slice(at, at + chunk)
        pulled = jnp.dot(turned_ref[rows, :], moved, preferred_element_type=F32)
        state = ready(rows)[1]
        new = decay_of(factor_scr[rows, :], coeff) * m_scr[rows, :] + 0.5 * (state * pulled)
        write(rows, new)
    return weights


def first_kernel(
    moved_ref, turned_ref, kappa_ref, coeff_ref, mask_ref, next_ref, traj_ref,
    low_ref, high_ref, edge_ref, weights_ref, m_scr, r_scr, factor_scr, wait,
):
    freqs, height, lon = moved_ref.shape
    points = 2 * lon
    directions = height // 2
    for f in range(freqs):
        block = moved_ref[f].astype(F32)
        rows = slice(f * directions, (f + 1) * directions)
        m_scr[rows, 0:lon] = block[0:directions]
        m_scr[rows, lon:points] = block[directions:height]
    r_scr[...] = m_scr[...].astype(BF16)
    wait(2, 3, 4)
    spread_factor(kappa_ref, factor_scr)
    mask = mask_ref[pl.ds(2 * lax.axis_index("freq"), 2), :].astype(F32)
    wait(5, 6)

    def ready(rows):
        return next_ref[rows, :], traj_ref[rows, :].astype(F32)

    def write(rows, values):
        low = (values[:, 0:lon] * mask[0:1]).astype(BF16)
        high = (values[:, lon:points] * mask[1:2]).astype(BF16)
        low_ref[rows, :] = low
        high_ref[rows, :] = high

    weights_ref[...] = two_substeps(
        m_scr, r_scr, turned_ref, factor_scr, coeff_ref[...], ready, write, True
    )
    picks = edge_picks(points, lon)
    edges = take_edges(low_ref[...], picks[:, 0:lon]) + take_edges(high_ref[...], picks[:, lon:points])
    edge_ref[...] = edges.astype(BF16)


def halo_kernel(
    low_ref, high_ref, north_ref, south_ref, west_ref, east_ref, rates_ref, pull_ref, own_ref, sed_ref,
    moved_ref, sums_ref, wait,
):
    components, lon = low_ref.shape
    cols = put_edges(west_ref[...], east_ref[...], 2 * lon, lon)
    weights = [own_ref[:, 0:lon], own_ref[:, lon : 2 * lon]]
    chunk = 144
    lane = lax.broadcasted_iota(jnp.int32, (chunk, lon), 1)
    for rows in blocks_of(components, components // chunk):
        low, high = low_ref[rows, :].astype(F32), high_ref[rows, :].astype(F32)
        above, below = north_ref[rows, :].astype(F32), south_ref[rows, :].astype(F32)
        rates = split_rates(rates_ref[0, rows, :], rates_ref[1, rows, :])
        for half, (here, up, down) in enumerate(((low, high, below), (high, above, low))):
            lanes = slice(half * lon, (half + 1) * lon)
            edge = cols[rows, lanes]
            east = jnp.where(lane == lon - 1, edge, pltpu.roll(here, lon - 1, 1))
            west = jnp.where(lane == 0, edge, pltpu.roll(here, 1, 1))
            value = (
                rates[0] * here
                + rates[1] * east
                + rates[2] * west
                + rates[3] * up
                + rates[4] * down
            ).astype(BF16)
            moved_ref[rows, lanes] = value
            terms = value.astype(F32) * pull_ref[rows, lanes].astype(F32)
            weights[half] = weights[half] + terms.reshape(chunk // 8, 8, lon).sum(axis=0)
    wait(9)
    groups, points = sums_ref.shape[2], 2 * lon
    hits = (lax.broadcasted_iota(jnp.int32, (groups, points), 0) == sed_ref[...]).astype(F32)
    sums = lax.dot_general(
        jnp.concatenate(weights, axis=1), hits, (((1,), (1,)), ((), ())),
        precision=lax.Precision.HIGHEST, preferred_element_type=F32,
    )
    sums_ref[...] = jnp.broadcast_to(sums.sum(axis=0, keepdims=True)[None], sums_ref.shape)


def last_kernel(
    moved_ref, turned_ref, kappa_ref, coeff_ref, next_ref, traj_ref, out_ref,
    m_scr, r_scr, factor_scr, wait,
):
    r_scr[...] = moved_ref[...]
    m_scr[...] = moved_ref[...].astype(F32)
    wait(2, 3)
    spread_factor(kappa_ref, factor_scr)
    wait(4, 5)

    def ready(rows):
        return next_ref[rows, :], traj_ref[rows, :].astype(F32)

    def write(rows, values):
        out_ref[rows, :] = values.astype(BF16)

    two_substeps(m_scr, r_scr, turned_ref, factor_scr, coeff_ref[...], ready, write, False)


def add_kernel(parts_ref, out_ref):
    out_ref[...] = jnp.broadcast_to(parts_ref[...].sum(axis=0)[None], out_ref.shape)


def final_kernel(scale, parts_ref, out_ref):
    out_ref[...] = parts_ref[...].sum(axis=0)[:, 0 : out_ref.shape[1]] * scale


def shards(
    adjoint_final, trajectory, interaction, friction_factor, friction_coeff,
    courant_lon, courant_lat, sea_mask, sediment,
):
    freq_local, directions, lat, lon = adjoint_final.shape
    steps, components, points = trajectory.shape
    groups = friction_coeff.shape[0]
    peers, regions = lax.axis_size("freq"), lax.axis_size("geo")
    rows = directions * lat
    height = rows // peers
    eastward = [(i, (i + 1) % regions) for i in range(regions)]
    westward = [(j, i) for i, j in eastward]
    northward = [(i, i + 1) for i in range(peers - 1)]
    southward = [(j, i) for i, j in northward]

    def swap(low, high, edges):
        return (
            lax.ppermute(low, "freq", southward),
            lax.ppermute(high, "freq", northward),
            lax.ppermute(edges, "geo", eastward),
            lax.ppermute(edges, "geo", westward),
        )

    field = adjoint_final.reshape(directions, lat, lon)
    grouped, edges, own_rates = call(
        regroup_kernel,
        [shape((rows + 2 * PAD, lon), F32), shape((16, rows), BF16), shape((2, height, lon), F32)],
        [field, sea_mask, courant_lon, courant_lat],
        late={0: None, 1: None, 2: None, 3: None},
    )
    from_west = lax.ppermute(edges, "geo", eastward)
    from_east = lax.ppermute(edges, "geo", westward)
    part, rate = call(
        functools.partial(interior_kernel, directions=directions),
        [shape((peers, height, lon), F32), shape((height, lon), F32)],
        [grouped, own_rates],
    )
    (sent,) = call(
        edges_kernel, [shape((peers, height, lon), BF16)], [part, rate, from_west, from_east]
    )
    sent, point_factor = lax.optimization_barrier((sent, friction_factor))
    moved = lax.all_to_all(sent, "freq", split_axis=0, concat_axis=0, tiled=True)

    product = 2 * components * components * points
    full, half_full = (components, points), (components, lon)
    coeff, next0, pull = call(
        pull_kernel,
        [shape((1, points), F32), shape(full, F32), shape(full, BF16)],
        [
            trajectory, interaction, point_factor, friction_coeff.reshape(1, groups),
            sediment.reshape(1, points),
        ],
        [pltpu.VMEM(full, F32), pltpu.VMEM(full, BF16)],
        flops=2 * product,
        late={2: None, 3: None, 4: None},
    )
    turned, next1, rates = call(
        states_kernel,
        [
            shape((components, components), BF16),
            shape(full, F32),
            shape((2, components, lon), F32),
        ],
        [trajectory, interaction, point_factor, coeff, courant_lon, courant_lat],
        [pltpu.VMEM(full, F32), pltpu.VMEM((128, 128), F32)],
        flops=product,
        late={2: None, 4: None, 5: None},
    )
    carried = [pltpu.VMEM(full, F32), pltpu.VMEM(full, BF16), pltpu.VMEM(full, F32)]
    low, high, edges, weights = call(
        first_kernel,
        [
            shape(half_full, BF16),
            shape(half_full, BF16),
            shape((16, components), BF16),
            shape((8, points), F32),
        ],
        [moved, turned, friction_factor, coeff, sea_mask, next1, trajectory],
        carried,
        flops=2 * product,
        late={2: None, 3: None, 4: None, 5: None, 6: 1},
    )
    moved, sums = call(
        halo_kernel,
        [shape(full, BF16), shape((peers, 1, 128), F32)],
        [
            low, high, *swap(low, high, edges), rates, pull, weights, sediment.reshape(1, points),
        ],
        late={9: None},
    )
    sums = lax.all_to_all(sums, "freq", split_axis=0, concat_axis=0, tiled=True)
    (result,) = call(
        last_kernel,
        [shape(full, BF16)],
        [moved, turned, friction_factor, coeff, next0, trajectory],
        carried,
        flops=2 * product,
        late={2: None, 3: None, 4: None, 5: 0},
    )
    result, sums = lax.optimization_barrier((result, sums))
    (sums,) = call(add_kernel, [shape((regions, 1, 128), F32)], [sums])
    sums = lax.all_to_all(sums, "geo", split_axis=0, concat_axis=0, tiled=True)
    point_total = points * peers * regions
    scale = -step_weight * groups / (point_total * components)
    (total,) = call(functools.partial(final_kernel, scale), [shape((1, groups), F32)], [sums])
    return result, total.reshape(groups)


def solution(mesh):
    in_specs = (
        P("freq", None, None, "geo"),
        P(None, None, ("geo", "freq")),
        P(),
        P(None, ("geo", "freq")),
        P(),
        P(),
        P(),
        P(None, "geo"),
        P(("geo", "freq")),
    )
    out_specs = (P(None, ("geo", "freq")), P())
    return jax.shard_map(shards, mesh=mesh, in_specs=in_specs, out_specs=out_specs, check_vma=False)
```

```python
import functools
import math

import jax
import jax.numpy as jnp
from jax import lax
from jax.experimental import pallas as pl
from jax.experimental.pallas import tpu as pltpu
from jax.sharding import PartitionSpec as P

F32 = jnp.float32
BF16 = jnp.bfloat16
step_weight = 0.25
PAD = 40
MIB = 1 << 20
WHOLE = pl.BlockSpec(memory_space=pltpu.VMEM)
OUTSIDE = pl.BlockSpec(memory_space=pl.ANY)


def call(kernel, outs, args, scratch=(), flops=0, late=None, outside_outs=(), limit=32):
    late = {} if late is None else late
    places = sorted(late)
    size = sum(a.size * a.dtype.itemsize for a in (*args, *outs))
    args = [
        pltpu.with_memory_space_constraint(a, pltpu.HBM) if i in late else a
        for i, a in enumerate(args)
    ]
    n = len(args) + len(outs) + len(scratch)

    def body(*refs):
        given, kept, buffers = list(refs[: len(args)]), refs[len(args) : n], refs[n:]
        copies = {}
        for k, i in enumerate(places):
            source = given[i] if late[i] is None else given[i].at[late[i]]
            copies[i] = pltpu.make_async_copy(source, buffers[k], buffers[-1].at[k])
            given[i] = buffers[k]
        for i in sorted(places, key=lambda i: math.prod(given[i].shape)):
            copies[i].start()
        if places:
            kernel(*given, *kept, wait=lambda *which: [copies[i].wait() for i in which])
        else:
            kernel(*given, *kept)

    buffers = [
        pltpu.VMEM(args[i].shape if late[i] is None else args[i].shape[1:], args[i].dtype)
        for i in places
    ]
    if places:
        buffers.append(pltpu.SemaphoreType.DMA((len(places),)))
    return pl.pallas_call(
        body,
        out_shape=outs,
        in_specs=[OUTSIDE if i in late else WHOLE for i in range(len(args))],
        out_specs=[OUTSIDE if i in outside_outs else WHOLE for i in range(len(outs))],
        scratch_shapes=[*scratch, *buffers],
        compiler_params=pltpu.CompilerParams(vmem_limit_bytes=limit * MIB),
        cost_estimate=pl.CostEstimate(flops=flops, bytes_accessed=size, transcendentals=0),
    )(*args)


def shape(dims, kind):
    return jax.ShapeDtypeStruct(dims, kind)


def edge_picks(width, lon):
    row = lax.broadcasted_iota(jnp.int32, (16, width), 0)
    lane = lax.broadcasted_iota(jnp.int32, (16, width), 1)
    picks = jnp.zeros((16, width), F32)
    for half in range(width // lon):
        picks = jnp.where((row == half) & (lane == half * lon), 1.0, picks)
        picks = jnp.where((row == 8 + half) & (lane == half * lon + lon - 1), 1.0, picks)
    return picks.astype(BF16)


def take_edges(values, picks):
    return lax.dot_general(picks, values, (((1,), (1,)), ((), ())), preferred_element_type=F32)


def put_edges(from_west, from_east, width, lon):
    both = jnp.concatenate([from_west.astype(F32), from_east.astype(F32)], axis=0).astype(BF16)
    return lax.dot_general(
        both, edge_picks(width, lon), (((0,), (0,)), ((), ())), preferred_element_type=F32
    )


def split_rates(lon_rate, lat_rate):
    lon_abs, lat_abs = jnp.abs(lon_rate), jnp.abs(lat_rate)
    east = jnp.where(lon_rate > 0, lon_abs, 0.0)
    north = jnp.where(lat_rate > 0, lat_abs, 0.0)
    return 1.0 - lon_abs - lat_abs, east, lon_abs - east, north, lat_abs - north


def regroup_kernel(
    field_ref, mask_ref, lon_ref, lat_ref, rows_ref, west_ref, east_ref, rates_ref, wait
):
    directions, lat, lon = field_ref.shape
    freqs = lon_ref.shape[0]
    rows = directions * lat
    height = rates_ref.shape[1]
    rows_ref[0:PAD, :] = jnp.zeros((PAD, lon), F32)
    rows_ref[PAD + rows :, :] = jnp.zeros((PAD, lon), F32)
    own = lax.broadcasted_iota(jnp.int32, (freqs, lon), 0) == lax.axis_index("freq")
    own = own.astype(F32)
    wait(2, 3)
    for at in range(0, height, directions):
        for slot, ref in enumerate((lon_ref, lat_ref)):
            rates_ref[slot, at : at + directions, :] = lax.dot_general(
                ref[...], own, (((0,), (0,)), ((), ())),
                precision=lax.Precision.HIGHEST, preferred_element_type=F32,
            )
    wait(0, 1)
    mask = mask_ref[...].astype(F32)
    for d in range(directions):
        rows_ref[pl.ds(PAD + d, lat, stride=directions), :] = field_ref[d].astype(F32) * mask
    edges = take_edges(rows_ref[PAD : PAD + rows, :].astype(BF16), edge_picks(lon, lon))
    west_ref[...] = edges[0:8].astype(BF16)
    east_ref[...] = edges[8:16].astype(BF16)


def interior_kernel(rows_ref, rates_ref, part_ref, rate_ref, *, directions):
    peers, height, lon = part_ref.shape
    center, east, west, north, south = split_rates(rates_ref[0], rates_ref[1])
    lane = lax.broadcasted_iota(jnp.int32, (height, lon), 1)
    rate_ref[...] = jnp.where(lane == 0, west, east)
    east = jnp.where(lane == lon - 1, 0.0, east)
    west = jnp.where(lane == 0, 0.0, west)
    for r in range(peers):
        at = PAD + r * height
        here = rows_ref[at : at + height, :]
        part_ref[r] = (
            center * here
            + east * pltpu.roll(here, lon - 1, 1)
            + west * pltpu.roll(here, 1, 1)
            + north * rows_ref[at + directions : at + directions + height, :]
            + south * rows_ref[at - directions : at - directions + height, :]
        )


def edges_kernel(part_ref, rate_ref, west_ref, east_ref, out_any, out_ref, sems):
    peers, height, lon = part_ref.shape
    groups = blocks_of(peers, 4)
    copies = []
    cols = put_edges(west_ref[...], east_ref[...], lon, lon)
    rate = rate_ref[...]
    for i, group in enumerate(groups):
        for r in range(group.start, group.stop):
            out_ref[r] = (part_ref[r] + rate * cols[r * height : (r + 1) * height]).astype(BF16)
        copies.append(pltpu.make_async_copy(out_ref.at[group], out_any.at[group], sems.at[i]))
        copies[-1].start()
    for copy in copies:
        copy.wait()


def spread_rates(courant_refs, turn_scr, rates_scr):
    freqs, directions = courant_refs[0].shape
    for slot, ref in enumerate(courant_refs):
        turn_scr[...] = jnp.zeros_like(turn_scr)
        turn_scr[0:freqs, 0:directions] = ref[...]
        turned = turn_scr[...].T
        for f in range(freqs):
            rates_scr[slot, f * directions : (f + 1) * directions, :] = jnp.broadcast_to(
                turned[0:directions, f : f + 1], (directions, rates_scr.shape[2])
            )


def spread_factor(kappa_ref, factor_scr):
    freqs, points = kappa_ref.shape
    directions = factor_scr.shape[0] // freqs
    for f in range(freqs):
        factor_scr[f * directions : (f + 1) * directions, :] = jnp.broadcast_to(
            kappa_ref[f : f + 1, :], (directions, points)
        )


def decay_of(factor, coeff):
    return 1.0 - step_weight * (factor * coeff)


def forward(state_ref, inter_ref, factor_scr, coeff, rows):
    forced = jnp.dot(inter_ref[rows, :], square_of(state_ref), preferred_element_type=F32)
    here = state_ref[rows, :].astype(F32)
    return here, decay_of(factor_scr[rows, :], coeff) * here + step_weight * forced


def square_of(state_ref):
    state = state_ref[...]
    return state * state


def blocks_of(size, count):
    return [slice(at, at + size // count) for at in range(0, size, size // count)]


def pull_kernel(
    trajectory_ref, inter_ref, kappa_ref, coeff_ref, sed_ref,
    point_coeff_ref, next_ref, pull_ref, factor_scr, product_scr, wait,
):
    traj_ref = trajectory_ref.at[0]
    components, points = traj_ref.shape
    groups = coeff_ref.shape[1]
    blocks = blocks_of(components, 4)
    wait(2, 3, 4)
    sediment = sed_ref[...]
    hits = (lax.broadcasted_iota(jnp.int32, (groups, points), 0) == sediment).astype(F32)
    coeff = jnp.dot(
        jnp.broadcast_to(coeff_ref[...], (8, groups)), hits,
        precision=lax.Precision.HIGHEST, preferred_element_type=F32,
    )[0:1]
    point_coeff_ref[...] = coeff
    spread_factor(kappa_ref, factor_scr)
    for rows in blocks:
        here, after = forward(traj_ref, inter_ref, factor_scr, coeff, rows)
        next_ref[rows, :] = after
        product_scr[rows, :] = (0.5 * factor_scr[rows, :] * here * after).astype(BF16)
    product = product_scr[...]
    for rows in blocks:
        pushed = jnp.dot(inter_ref[rows, :], product, preferred_element_type=F32)
        factor, here = factor_scr[rows, :], traj_ref[rows, :].astype(F32)
        pull = factor * (next_ref[rows, :] + decay_of(factor, coeff) * here) + pushed
        pull_ref[rows, :] = pull.astype(BF16)


def states_kernel(
    trajectory_ref, inter_ref, kappa_ref, coeff_ref, courant_lon_ref, courant_lat_ref,
    turned_ref, next_ref, rates_ref, factor_scr, turn_scr, wait,
):
    traj_ref = trajectory_ref.at[1]
    components = traj_ref.shape[0]
    wait(2, 4, 5)
    spread_factor(kappa_ref, factor_scr)
    spread_rates((courant_lon_ref, courant_lat_ref), turn_scr, rates_ref)
    coeff = coeff_ref[...]
    turned_ref[...] = inter_ref[...].T
    for rows in blocks_of(components, 4):
        next_ref[rows, :] = forward(traj_ref, inter_ref, factor_scr, coeff, rows)[1]


def two_substeps(carried, turned_ref, kappa_ref, prepare, ready, write, weigh):
    m_scr, r_scr, factor_scr, product_scr = carried
    components, points = m_scr.shape
    blocks = blocks_of(components, 4)
    weights = jnp.zeros((8, points), F32)
    moved = r_scr[...]
    for rows in blocks:
        product_scr[rows, :] = jnp.dot(turned_ref[rows, :], moved, preferred_element_type=F32)
    coeff = prepare()
    spread_factor(kappa_ref, factor_scr)
    for rows in blocks:
        after, state = ready(rows)
        factor, old = factor_scr[rows, :], m_scr[rows, :]
        new = decay_of(factor, coeff) * old + 0.5 * (after * product_scr[rows, :])
        if weigh:
            terms = factor * (old * after + new * state)
            weights = weights + terms.reshape(-1, 8, points).sum(axis=0)
        m_scr[rows, :] = new
        r_scr[rows, :] = new.astype(BF16)
    moved = r_scr[...]
    for rows in blocks:
        pulled = jnp.dot(turned_ref[rows, :], moved, preferred_element_type=F32)
        state = ready(rows)[1]
        new = decay_of(factor_scr[rows, :], coeff) * m_scr[rows, :] + 0.5 * (state * pulled)
        write(rows, new)
    return weights


def first_kernel(
    moved_ref, turned_ref, kappa_ref, coeff_ref, mask_ref, next_ref, traj_ref,
    low_ref, high_ref, west_ref, east_ref, weights_ref, *carried, wait,
):
    freqs, height, lon = moved_ref.shape
    points = 2 * lon
    directions = height // 2
    m_scr, r_scr = carried[:2]
    for f in range(freqs):
        block = moved_ref[f].astype(F32)
        rows = slice(f * directions, (f + 1) * directions)
        m_scr[rows, 0:lon] = block[0:directions]
        m_scr[rows, lon:points] = block[directions:height]
    r_scr[...] = m_scr[...].astype(BF16)

    def prepare():
        wait(2, 3, 5, 6)
        return coeff_ref[...]

    def masks():
        return mask_ref[pl.ds(2 * lax.axis_index("freq"), 2), :].astype(F32)

    def ready(rows):
        return next_ref[rows, :], traj_ref[rows, :].astype(F32)

    def write(rows, values):
        if rows.start == 0:
            wait(4)
        mask = masks()
        low = (values[:, 0:lon] * mask[0:1]).astype(BF16)
        high = (values[:, lon:points] * mask[1:2]).astype(BF16)
        low_ref[rows, :] = low
        high_ref[rows, :] = high

    weights_ref[...] = two_substeps(
        carried, turned_ref, kappa_ref, prepare, ready, write, True
    )
    picks = edge_picks(points, lon)
    edges = take_edges(low_ref[...], picks[:, 0:lon]) + take_edges(high_ref[...], picks[:, lon:points])
    west_ref[...] = edges[0:8].astype(BF16)
    east_ref[...] = edges[8:16].astype(BF16)


def inner_kernel(
    low_ref, high_ref, courant_ref, part_ref, edge_rate_ref, north_rate_ref, south_rate_ref
):
    components, lon = low_ref.shape
    chunk = 144
    lane = lax.broadcasted_iota(jnp.int32, (chunk, lon), 1)
    for rows in blocks_of(components, components // chunk):
        low, high = low_ref[rows, :].astype(F32), high_ref[rows, :].astype(F32)
        center, east, west, north, south = split_rates(
            courant_ref[0, rows, :], courant_ref[1, rows, :]
        )
        edge_rate_ref[rows, :] = jnp.where(lane == 0, west, east)
        north_rate_ref[rows, :] = north
        south_rate_ref[rows, :] = south
        east = jnp.where(lane == lon - 1, 0.0, east)
        west = jnp.where(lane == 0, 0.0, west)
        for half, (here, rate, other) in enumerate(((low, north, high), (high, south, low))):
            part_ref[rows, half * lon : (half + 1) * lon] = (
                center * here
                + east * pltpu.roll(here, lon - 1, 1)
                + west * pltpu.roll(here, 1, 1)
                + rate * other
            )


def halo_kernel(
    part_ref, edge_rate_ref, north_rate_ref, south_rate_ref, north_ref, south_ref, west_ref, east_ref,
    pull_ref, own_ref, sed_ref, moved_ref, sums_ref, wait,
):
    components, lon = north_ref.shape
    cols = put_edges(west_ref[...], east_ref[...], 2 * lon, lon)
    weights = [own_ref[:, 0:lon], own_ref[:, lon : 2 * lon]]
    for rows in blocks_of(components, components // 144):
        edge_rate = edge_rate_ref[rows, :]
        below = south_rate_ref[rows, :] * south_ref[rows, :].astype(F32)
        above = north_rate_ref[rows, :] * north_ref[rows, :].astype(F32)
        for half, outer in enumerate((below, above)):
            lanes = slice(half * lon, (half + 1) * lon)
            value = (part_ref[rows, lanes] + outer + edge_rate * cols[rows, lanes]).astype(BF16)
            moved_ref[rows, lanes] = value
            terms = value.astype(F32) * pull_ref[rows, lanes].astype(F32)
            weights[half] = weights[half] + terms.reshape(-1, 8, lon).sum(axis=0)
    wait(10)
    groups, points = sums_ref.shape[2], 2 * lon
    hits = (lax.broadcasted_iota(jnp.int32, (groups, points), 0) == sed_ref[...]).astype(F32)
    sums = lax.dot_general(
        jnp.concatenate(weights, axis=1), hits, (((1,), (1,)), ((), ())),
        precision=lax.Precision.HIGHEST, preferred_element_type=F32,
    )
    sums_ref[...] = jnp.broadcast_to(sums.sum(axis=0, keepdims=True)[None], sums_ref.shape)


def last_kernel(
    moved_ref, turned_ref, kappa_ref, coeff_ref, next_ref, traj_ref, out_any, *carried, wait
):
    *carried, out_ref, sems = carried
    copies = []
    m_scr, r_scr = carried[:2]
    r_scr[...] = moved_ref[...]
    m_scr[...] = moved_ref[...].astype(F32)

    def prepare():
        wait(2, 3, 4, 5)
        return coeff_ref[...]

    def ready(rows):
        return next_ref[rows, :], traj_ref[rows, :].astype(F32)

    def write(rows, values):
        out_ref[rows, :] = values.astype(BF16)
        copies.append(
            pltpu.make_async_copy(out_ref.at[rows, :], out_any.at[rows, :], sems.at[len(copies)])
        )
        copies[-1].start()

    two_substeps(carried, turned_ref, kappa_ref, prepare, ready, write, False)
    for copy in copies:
        copy.wait()


def add_kernel(parts_ref, out_ref):
    out_ref[...] = jnp.broadcast_to(parts_ref[...].sum(axis=0)[None], out_ref.shape)


def final_kernel(scale, parts_ref, out_ref):
    out_ref[...] = parts_ref[...].sum(axis=0)[:, 0 : out_ref.shape[1]] * scale


def shards(
    adjoint_final, trajectory, interaction, friction_factor, friction_coeff,
    courant_lon, courant_lat, sea_mask, sediment,
):
    freq_local, directions, lat, lon = adjoint_final.shape
    steps, components, points = trajectory.shape
    groups = friction_coeff.shape[0]
    peers, regions = lax.axis_size("freq"), lax.axis_size("geo")
    rows = directions * lat
    height = rows // peers
    eastward = [(i, (i + 1) % regions) for i in range(regions)]
    westward = [(j, i) for i, j in eastward]
    northward = [(i, i + 1) for i in range(peers - 1)]
    southward = [(j, i) for i, j in northward]

    def swap(low, high, west, east):
        return (
            lax.ppermute(low, "freq", southward),
            lax.ppermute(high, "freq", northward),
            lax.ppermute(east, "geo", eastward),
            lax.ppermute(west, "geo", westward),
        )

    field = adjoint_final.reshape(directions, lat, lon)
    grouped, west, east, own_rates = call(
        regroup_kernel,
        [
            shape((rows + 2 * PAD, lon), F32),
            shape((8, rows), BF16),
            shape((8, rows), BF16),
            shape((2, height, lon), F32),
        ],
        [field, sea_mask, courant_lon, courant_lat],
        late={0: None, 1: None, 2: None, 3: None},
    )
    from_west = lax.ppermute(east, "geo", eastward)
    from_east = lax.ppermute(west, "geo", westward)
    part, rate = call(
        functools.partial(interior_kernel, directions=directions),
        [shape((peers, height, lon), F32), shape((height, lon), F32)],
        [grouped, own_rates],
    )
    (sent,) = call(
        edges_kernel,
        [shape((peers, height, lon), BF16)],
        [part, rate, from_west, from_east],
        [pltpu.VMEM((peers, height, lon), BF16), pltpu.SemaphoreType.DMA((4,))],
        outside_outs=(0,),
    )
    sent, point_factor = lax.optimization_barrier((sent, friction_factor))
    moved = lax.all_to_all(sent, "freq", split_axis=0, concat_axis=0, tiled=True)

    product = 2 * components * components * points
    full, half_full = (components, points), (components, lon)
    coeff, next0, pull = call(
        pull_kernel,
        [shape((1, points), F32), shape(full, F32), shape(full, BF16)],
        [
            trajectory, interaction, point_factor, friction_coeff.reshape(1, groups),
            sediment.reshape(1, points),
        ],
        [pltpu.VMEM(full, F32), pltpu.VMEM(full, BF16)],
        flops=2 * product,
        late={2: None, 3: None, 4: None},
    )
    turned, next1, rates = call(
        states_kernel,
        [
            shape((components, components), BF16),
            shape(full, F32),
            shape((2, components, lon), F32),
        ],
        [trajectory, interaction, point_factor, coeff, courant_lon, courant_lat],
        [pltpu.VMEM(full, F32), pltpu.VMEM((128, 128), F32)],
        flops=product,
        late={2: None, 4: None, 5: None},
    )
    carried = [pltpu.VMEM(full, kind) for kind in (F32, BF16, F32, F32)]
    low, high, west, east, weights = call(
        first_kernel,
        [
            shape(half_full, BF16),
            shape(half_full, BF16),
            shape((8, components), BF16),
            shape((8, components), BF16),
            shape((8, points), F32),
        ],
        [moved, turned, friction_factor, coeff, sea_mask, next1, trajectory],
        carried,
        flops=2 * product,
        late={2: None, 3: None, 4: None, 5: None, 6: 1},
    )
    swapped = swap(low, high, west, east)
    inner = call(
        inner_kernel,
        [shape(full, F32), shape(half_full, F32), shape(half_full, F32), shape(half_full, F32)],
        [low, high, rates],
    )
    moved, sums = call(
        halo_kernel,
        [shape(full, BF16), shape((peers, 1, 128), F32)],
        [*inner, *swapped, pull, weights, sediment.reshape(1, points)],
        late={10: None},
    )
    sums = lax.all_to_all(sums, "freq", split_axis=0, concat_axis=0, tiled=True)
    (result,) = call(
        last_kernel,
        [shape(full, BF16)],
        [moved, turned, friction_factor, coeff, next0, trajectory],
        [*carried, pltpu.VMEM(full, BF16), pltpu.SemaphoreType.DMA((4,))],
        flops=2 * product,
        late={2: None, 3: None, 4: None, 5: 0},
        outside_outs=(0,),
    )
    result, sums = lax.optimization_barrier((result, sums))
    (sums,) = call(add_kernel, [shape((regions, 1, 128), F32)], [sums])
    sums = lax.all_to_all(sums, "geo", split_axis=0, concat_axis=0, tiled=True)
    point_total = points * peers * regions
    scale = -step_weight * groups / (point_total * components)
    (total,) = call(functools.partial(final_kernel, scale), [shape((1, groups), F32)], [sums])
    return result, total.reshape(groups)


def solution(mesh):
    in_specs = (
        P("freq", None, None, "geo"),
        P(None, None, ("geo", "freq")),
        P(),
        P(None, ("geo", "freq")),
        P(),
        P(),
        P(),
        P(None, "geo"),
        P(("geo", "freq")),
    )
    out_specs = (P(None, ("geo", "freq")), P())
    return jax.shard_map(shards, mesh=mesh, in_specs=in_specs, out_specs=out_specs, check_vma=False)
```

```python
import functools
import math

import jax
import jax.numpy as jnp
from jax import lax
from jax.experimental import pallas as pl
from jax.experimental.pallas import tpu as pltpu
from jax.sharding import PartitionSpec as P

F32 = jnp.float32
BF16 = jnp.bfloat16
step_weight = 0.25
PAD = 40
MIB = 1 << 20
PARTS = 4
WHOLE = pl.BlockSpec(memory_space=pltpu.VMEM)
OUTSIDE = pl.BlockSpec(memory_space=pl.ANY)


def call(kernel, outs, args, scratch=(), flops=0, late=None, parted=(), outside_outs=(), limit=32):
    late = {} if late is None else late
    places = sorted(late)
    size = sum(a.size * a.dtype.itemsize for a in (*args, *outs))
    args = [
        pltpu.with_memory_space_constraint(a, pltpu.HBM) if i in late else a
        for i, a in enumerate(args)
    ]
    n = len(args) + len(outs) + len(scratch)

    def body(*refs):
        given, kept, buffers = list(refs[: len(args)]), refs[len(args) : n], refs[n:]
        copies, sources = {}, {}
        order = sorted(range(len(places)), key=lambda k: math.prod(buffers[k].shape))
        for k in order:
            i = places[k]
            source = given[i] if late[i] is None else given[i].at[late[i]]
            sources[i], given[i] = source, buffers[k]
            if i not in parted:
                copies[i] = pltpu.make_async_copy(source, buffers[k], buffers[-1].at[k, 0])
                copies[i].start()
        for part in range(PARTS):
            for k in order:
                i = places[k]
                if i in parted:
                    source = sources[i]
                    rows = blocks_of(source.shape[0], PARTS)[part]
                    copies[i, part] = pltpu.make_async_copy(
                        source.at[rows, :], buffers[k].at[rows, :], buffers[-1].at[k, part]
                    )
                    copies[i, part].start()
        if places:
            kernel(*given, *kept, wait=lambda *which: [copies[i].wait() for i in which])
        else:
            kernel(*given, *kept)

    buffers = [
        pltpu.VMEM(args[i].shape if late[i] is None else args[i].shape[1:], args[i].dtype)
        for i in places
    ]
    if places:
        buffers.append(pltpu.SemaphoreType.DMA((len(places), PARTS)))
    return pl.pallas_call(
        body,
        out_shape=outs,
        in_specs=[OUTSIDE if i in late else WHOLE for i in range(len(args))],
        out_specs=[OUTSIDE if i in outside_outs else WHOLE for i in range(len(outs))],
        scratch_shapes=[*scratch, *buffers],
        compiler_params=pltpu.CompilerParams(vmem_limit_bytes=limit * MIB),
        cost_estimate=pl.CostEstimate(flops=flops, bytes_accessed=size, transcendentals=0),
    )(*args)


def shape(dims, kind):
    return jax.ShapeDtypeStruct(dims, kind)


def edge_picks(width, lon):
    row = lax.broadcasted_iota(jnp.int32, (16, width), 0)
    lane = lax.broadcasted_iota(jnp.int32, (16, width), 1)
    picks = jnp.zeros((16, width), F32)
    for half in range(width // lon):
        picks = jnp.where((row == half) & (lane == half * lon), 1.0, picks)
        picks = jnp.where((row == 8 + half) & (lane == half * lon + lon - 1), 1.0, picks)
    return picks.astype(BF16)


def take_edges(values, picks):
    return lax.dot_general(picks, values, (((1,), (1,)), ((), ())), preferred_element_type=F32)


def put_edges(from_west, from_east, width, lon):
    both = jnp.concatenate([from_west.astype(F32), from_east.astype(F32)], axis=0).astype(BF16)
    return lax.dot_general(
        both, edge_picks(width, lon), (((0,), (0,)), ((), ())), preferred_element_type=F32
    )


def split_rates(lon_rate, lat_rate):
    lon_abs, lat_abs = jnp.abs(lon_rate), jnp.abs(lat_rate)
    east = jnp.where(lon_rate > 0, lon_abs, 0.0)
    north = jnp.where(lat_rate > 0, lat_abs, 0.0)
    return 1.0 - lon_abs - lat_abs, east, lon_abs - east, north, lat_abs - north


def regroup_kernel(
    field_ref, mask_ref, lon_ref, lat_ref, rows_ref, west_ref, east_ref, rates_ref, wait
):
    directions, lat, lon = field_ref.shape
    freqs = lon_ref.shape[0]
    rows = directions * lat
    height = rates_ref.shape[1]
    rows_ref[0:PAD, :] = jnp.zeros((PAD, lon), F32)
    rows_ref[PAD + rows :, :] = jnp.zeros((PAD, lon), F32)
    own = lax.broadcasted_iota(jnp.int32, (freqs, lon), 0) == lax.axis_index("freq")
    own = own.astype(F32)
    wait(2, 3)
    for at in range(0, height, directions):
        for slot, ref in enumerate((lon_ref, lat_ref)):
            rates_ref[slot, at : at + directions, :] = lax.dot_general(
                ref[...], own, (((0,), (0,)), ((), ())),
                precision=lax.Precision.HIGHEST, preferred_element_type=F32,
            )
    wait(0, 1)
    mask = mask_ref[...].astype(F32)
    for d in range(directions):
        rows_ref[pl.ds(PAD + d, lat, stride=directions), :] = field_ref[d].astype(F32) * mask
    edges = take_edges(rows_ref[PAD : PAD + rows, :].astype(BF16), edge_picks(lon, lon))
    west_ref[...] = edges[0:8].astype(BF16)
    east_ref[...] = edges[8:16].astype(BF16)


def interior_kernel(rows_ref, rates_ref, part_ref, rate_ref, *, directions):
    peers, height, lon = part_ref.shape
    center, east, west, north, south = split_rates(rates_ref[0], rates_ref[1])
    lane = lax.broadcasted_iota(jnp.int32, (height, lon), 1)
    rate_ref[...] = jnp.where(lane == 0, west, east)
    east = jnp.where(lane == lon - 1, 0.0, east)
    west = jnp.where(lane == 0, 0.0, west)
    for r in range(peers):
        at = PAD + r * height
        here = rows_ref[at : at + height, :]
        part_ref[r] = (
            center * here
            + east * pltpu.roll(here, lon - 1, 1)
            + west * pltpu.roll(here, 1, 1)
            + north * rows_ref[at + directions : at + directions + height, :]
            + south * rows_ref[at - directions : at - directions + height, :]
        )


def edges_kernel(part_ref, rate_ref, west_ref, east_ref, out_any, out_ref, sems):
    peers, height, lon = part_ref.shape
    groups = blocks_of(peers, 4)
    copies = []
    cols = put_edges(west_ref[...], east_ref[...], lon, lon)
    rate = rate_ref[...]
    for i, group in enumerate(groups):
        for r in range(group.start, group.stop):
            out_ref[r] = (part_ref[r] + rate * cols[r * height : (r + 1) * height]).astype(BF16)
        copies.append(pltpu.make_async_copy(out_ref.at[group], out_any.at[group], sems.at[i]))
        copies[-1].start()
    for copy in copies:
        copy.wait()


def spread_rates(courant_refs, turn_scr, rates_scr):
    freqs, directions = courant_refs[0].shape
    for slot, ref in enumerate(courant_refs):
        turn_scr[...] = jnp.zeros_like(turn_scr)
        turn_scr[0:freqs, 0:directions] = ref[...]
        turned = turn_scr[...].T
        for f in range(freqs):
            rates_scr[slot, f * directions : (f + 1) * directions, :] = jnp.broadcast_to(
                turned[0:directions, f : f + 1], (directions, rates_scr.shape[2])
            )


def spread_factor(kappa_ref, factor_scr):
    freqs, points = kappa_ref.shape
    directions = factor_scr.shape[0] // freqs
    for f in range(freqs):
        factor_scr[f * directions : (f + 1) * directions, :] = jnp.broadcast_to(
            kappa_ref[f : f + 1, :], (directions, points)
        )


def decay_of(factor, coeff):
    return 1.0 - step_weight * (factor * coeff)


def forward(state_ref, inter_ref, factor_scr, coeff, rows):
    forced = jnp.dot(inter_ref[rows, :], square_of(state_ref), preferred_element_type=F32)
    here = state_ref[rows, :].astype(F32)
    return here, decay_of(factor_scr[rows, :], coeff) * here + step_weight * forced


def square_of(state_ref):
    state = state_ref[...]
    return state * state


def blocks_of(size, count):
    return [slice(at, at + size // count) for at in range(0, size, size // count)]


def pull_kernel(
    trajectory_ref, inter_ref, kappa_ref, coeff_ref, sed_ref,
    point_coeff_ref, next_ref, pull_ref, factor_scr, product_scr, wait,
):
    traj_ref = trajectory_ref.at[0]
    components, points = traj_ref.shape
    groups = coeff_ref.shape[1]
    blocks = blocks_of(components, 4)
    wait(2, 3, 4)
    sediment = sed_ref[...]
    hits = (lax.broadcasted_iota(jnp.int32, (groups, points), 0) == sediment).astype(F32)
    coeff = jnp.dot(
        jnp.broadcast_to(coeff_ref[...], (8, groups)), hits,
        precision=lax.Precision.HIGHEST, preferred_element_type=F32,
    )[0:1]
    point_coeff_ref[...] = coeff
    spread_factor(kappa_ref, factor_scr)
    for rows in blocks:
        here, after = forward(traj_ref, inter_ref, factor_scr, coeff, rows)
        next_ref[rows, :] = after
        product_scr[rows, :] = (0.5 * factor_scr[rows, :] * here * after).astype(BF16)
    product = product_scr[...]
    for rows in blocks:
        pushed = jnp.dot(inter_ref[rows, :], product, preferred_element_type=F32)
        factor, here = factor_scr[rows, :], traj_ref[rows, :].astype(F32)
        pull = factor * (next_ref[rows, :] + decay_of(factor, coeff) * here) + pushed
        pull_ref[rows, :] = pull.astype(BF16)


def states_kernel(
    trajectory_ref, inter_ref, kappa_ref, coeff_ref, courant_lon_ref, courant_lat_ref,
    turned_ref, next_ref, rates_ref, factor_scr, turn_scr, wait,
):
    traj_ref = trajectory_ref.at[1]
    components = traj_ref.shape[0]
    wait(2, 4, 5)
    spread_factor(kappa_ref, factor_scr)
    spread_rates((courant_lon_ref, courant_lat_ref), turn_scr, rates_ref)
    coeff = coeff_ref[...]
    turned_ref[...] = inter_ref[...].T
    for rows in blocks_of(components, 4):
        next_ref[rows, :] = forward(traj_ref, inter_ref, factor_scr, coeff, rows)[1]


def two_substeps(carried, turned_ref, kappa_ref, prepare, ready, write, weigh):
    m_scr, r_scr, factor_scr, product_scr = carried
    components, points = m_scr.shape
    blocks = blocks_of(components, PARTS)
    weights = jnp.zeros((8, points), F32)
    moved = r_scr[...]
    for rows in blocks:
        product_scr[rows, :] = jnp.dot(turned_ref[rows, :], moved, preferred_element_type=F32)
    coeff = prepare()
    spread_factor(kappa_ref, factor_scr)
    for rows in blocks:
        after, state = ready(rows)
        factor, old = factor_scr[rows, :], m_scr[rows, :]
        new = decay_of(factor, coeff) * old + 0.5 * (after * product_scr[rows, :])
        if weigh:
            terms = factor * (old * after + new * state)
            weights = weights + terms.reshape(-1, 8, points).sum(axis=0)
        m_scr[rows, :] = new
        r_scr[rows, :] = new.astype(BF16)
    moved = r_scr[...]
    for rows in blocks:
        pulled = jnp.dot(turned_ref[rows, :], moved, preferred_element_type=F32)
        state = ready(rows)[1]
        new = decay_of(factor_scr[rows, :], coeff) * m_scr[rows, :] + 0.5 * (state * pulled)
        write(rows, new)
    return weights


def first_kernel(
    moved_ref, turned_ref, kappa_ref, coeff_ref, mask_ref, next_ref, traj_ref,
    low_ref, high_ref, edge_ref, weights_ref, *carried, wait,
):
    freqs, height, lon = moved_ref.shape
    points = 2 * lon
    directions = height // 2
    m_scr, r_scr = carried[:2]
    for f in range(freqs):
        block = moved_ref[f].astype(F32)
        rows = slice(f * directions, (f + 1) * directions)
        m_scr[rows, 0:lon] = block[0:directions]
        m_scr[rows, lon:points] = block[directions:height]
    r_scr[...] = m_scr[...].astype(BF16)

    def prepare():
        wait(2, 3)
        return coeff_ref[...]

    def masks():
        return mask_ref[pl.ds(2 * lax.axis_index("freq"), 2), :].astype(F32)

    unread = list(range(PARTS))

    def ready(rows):
        if unread:
            part = unread.pop(0)
            wait((5, part), (6, part))
        return next_ref[rows, :], traj_ref[rows, :].astype(F32)

    def write(rows, values):
        if rows.start == 0:
            wait(4)
        mask = masks()
        low = (values[:, 0:lon] * mask[0:1]).astype(BF16)
        high = (values[:, lon:points] * mask[1:2]).astype(BF16)
        low_ref[rows, :] = low
        high_ref[rows, :] = high

    weights_ref[...] = two_substeps(
        carried, turned_ref, kappa_ref, prepare, ready, write, True
    )
    picks = edge_picks(points, lon)
    edges = take_edges(low_ref[...], picks[:, 0:lon]) + take_edges(high_ref[...], picks[:, lon:points])
    edge_ref[...] = edges.astype(BF16)


def inner_kernel(
    low_ref, high_ref, courant_ref, part_ref, edge_rate_ref, north_rate_ref, south_rate_ref
):
    components, lon = low_ref.shape
    chunk = 144
    lane = lax.broadcasted_iota(jnp.int32, (chunk, lon), 1)
    for rows in blocks_of(components, components // chunk):
        low, high = low_ref[rows, :].astype(F32), high_ref[rows, :].astype(F32)
        center, east, west, north, south = split_rates(
            courant_ref[0, rows, :], courant_ref[1, rows, :]
        )
        edge_rate_ref[rows, :] = jnp.where(lane == 0, west, east)
        north_rate_ref[rows, :] = north
        south_rate_ref[rows, :] = south
        east = jnp.where(lane == lon - 1, 0.0, east)
        west = jnp.where(lane == 0, 0.0, west)
        for half, (here, rate, other) in enumerate(((low, north, high), (high, south, low))):
            part_ref[rows, half * lon : (half + 1) * lon] = (
                center * here
                + east * pltpu.roll(here, lon - 1, 1)
                + west * pltpu.roll(here, 1, 1)
                + rate * other
            )


def halo_kernel(
    part_ref, edge_rate_ref, north_rate_ref, south_rate_ref, north_ref, south_ref, west_ref, east_ref,
    pull_ref, own_ref, sed_ref, moved_ref, sums_ref, wait,
):
    components, lon = north_ref.shape
    cols = put_edges(west_ref[...].astype(F32)[8:16], east_ref[...].astype(F32)[0:8], 2 * lon, lon)
    weights = [own_ref[:, 0:lon], own_ref[:, lon : 2 * lon]]
    for rows in blocks_of(components, components // 144):
        edge_rate = edge_rate_ref[rows, :]
        below = south_rate_ref[rows, :] * south_ref[rows, :].astype(F32)
        above = north_rate_ref[rows, :] * north_ref[rows, :].astype(F32)
        for half, outer in enumerate((below, above)):
            lanes = slice(half * lon, (half + 1) * lon)
            value = (part_ref[rows, lanes] + outer + edge_rate * cols[rows, lanes]).astype(BF16)
            moved_ref[rows, lanes] = value
            terms = value.astype(F32) * pull_ref[rows, lanes].astype(F32)
            weights[half] = weights[half] + terms.reshape(-1, 8, lon).sum(axis=0)
    wait(10)
    groups, points = sums_ref.shape[2], 2 * lon
    hits = (lax.broadcasted_iota(jnp.int32, (groups, points), 0) == sed_ref[...]).astype(F32)
    sums = lax.dot_general(
        jnp.concatenate(weights, axis=1), hits, (((1,), (1,)), ((), ())),
        precision=lax.Precision.HIGHEST, preferred_element_type=F32,
    )
    sums_ref[...] = jnp.broadcast_to(sums.sum(axis=0, keepdims=True)[None], sums_ref.shape)


def last_kernel(
    moved_ref, turned_ref, kappa_ref, coeff_ref, next_ref, traj_ref, out_any, *carried, wait
):
    *carried, out_ref, sems = carried
    copies = []
    m_scr, r_scr = carried[:2]
    r_scr[...] = moved_ref[...]
    m_scr[...] = moved_ref[...].astype(F32)

    def prepare():
        wait(2, 3, 4, 5)
        return coeff_ref[...]

    def ready(rows):
        return next_ref[rows, :], traj_ref[rows, :].astype(F32)

    def write(rows, values):
        out_ref[rows, :] = values.astype(BF16)
        copies.append(
            pltpu.make_async_copy(out_ref.at[rows, :], out_any.at[rows, :], sems.at[len(copies)])
        )
        copies[-1].start()

    two_substeps(carried, turned_ref, kappa_ref, prepare, ready, write, False)
    for copy in copies:
        copy.wait()


def add_kernel(parts_ref, out_ref):
    out_ref[...] = jnp.broadcast_to(parts_ref[...].sum(axis=0)[None], out_ref.shape)


def final_kernel(scale, parts_ref, out_ref):
    out_ref[...] = parts_ref[...].sum(axis=0)[:, 0 : out_ref.shape[1]] * scale


def shards(
    adjoint_final, trajectory, interaction, friction_factor, friction_coeff,
    courant_lon, courant_lat, sea_mask, sediment,
):
    freq_local, directions, lat, lon = adjoint_final.shape
    steps, components, points = trajectory.shape
    groups = friction_coeff.shape[0]
    peers, regions = lax.axis_size("freq"), lax.axis_size("geo")
    rows = directions * lat
    height = rows // peers
    eastward = [(i, (i + 1) % regions) for i in range(regions)]
    westward = [(j, i) for i, j in eastward]
    northward = [(i, i + 1) for i in range(peers - 1)]
    southward = [(j, i) for i, j in northward]

    field = adjoint_final.reshape(directions, lat, lon)
    grouped, west, east, own_rates = call(
        regroup_kernel,
        [
            shape((rows + 2 * PAD, lon), F32),
            shape((8, rows), BF16),
            shape((8, rows), BF16),
            shape((2, height, lon), F32),
        ],
        [field, sea_mask, courant_lon, courant_lat],
        late={0: None, 1: None, 2: None, 3: None},
    )
    from_west = lax.ppermute(east, "geo", eastward)
    from_east = lax.ppermute(west, "geo", westward)
    part, rate = call(
        functools.partial(interior_kernel, directions=directions),
        [shape((peers, height, lon), F32), shape((height, lon), F32)],
        [grouped, own_rates],
    )
    (sent,) = call(
        edges_kernel,
        [shape((peers, height, lon), BF16)],
        [part, rate, from_west, from_east],
        [pltpu.VMEM((peers, height, lon), BF16), pltpu.SemaphoreType.DMA((4,))],
        outside_outs=(0,),
    )
    sent, point_factor = lax.optimization_barrier((sent, friction_factor))
    moved = lax.all_to_all(sent, "freq", split_axis=0, concat_axis=0, tiled=True)

    product = 2 * components * components * points
    full, half_full = (components, points), (components, lon)
    coeff, next0, pull = call(
        pull_kernel,
        [shape((1, points), F32), shape(full, F32), shape(full, BF16)],
        [
            trajectory, interaction, point_factor, friction_coeff.reshape(1, groups),
            sediment.reshape(1, points),
        ],
        [pltpu.VMEM(full, F32), pltpu.VMEM(full, BF16)],
        flops=2 * product,
        late={2: None, 3: None, 4: None},
    )
    turned, next1, rates = call(
        states_kernel,
        [
            shape((components, components), BF16),
            shape(full, F32),
            shape((2, components, lon), F32),
        ],
        [trajectory, interaction, point_factor, coeff, courant_lon, courant_lat],
        [pltpu.VMEM(full, F32), pltpu.VMEM((128, 128), F32)],
        flops=product,
        late={2: None, 4: None, 5: None},
    )
    carried = [pltpu.VMEM(full, kind) for kind in (F32, BF16, F32, F32)]
    low, high, edges, weights = call(
        first_kernel,
        [
            shape(half_full, BF16),
            shape(half_full, BF16),
            shape((16, components), BF16),
            shape((8, points), F32),
        ],
        [moved, turned, friction_factor, coeff, sea_mask, next1, trajectory],
        carried,
        flops=2 * product,
        late={2: None, 3: None, 4: None, 5: None, 6: 1},
        parted=(5, 6),
    )
    above = lax.ppermute(low, "freq", southward)
    below = lax.ppermute(high, "freq", northward)
    from_west = lax.ppermute(edges, "geo", eastward)
    from_east = lax.ppermute(edges, "geo", westward)
    inner = call(
        inner_kernel,
        [shape(full, F32), shape(half_full, F32), shape(half_full, F32), shape(half_full, F32)],
        [low, high, rates],
    )
    moved, sums = call(
        halo_kernel,
        [shape(full, BF16), shape((peers, 1, 128), F32)],
        [*inner, above, below, from_west, from_east, pull, weights, sediment.reshape(1, points)],
        late={10: None},
    )
    sums = lax.all_to_all(sums, "freq", split_axis=0, concat_axis=0, tiled=True)
    sums, moved = lax.optimization_barrier((sums, moved))
    (result,) = call(
        last_kernel,
        [shape(full, BF16)],
        [moved, turned, friction_factor, coeff, next0, trajectory],
        [*carried, pltpu.VMEM(full, BF16), pltpu.SemaphoreType.DMA((4,))],
        flops=2 * product,
        late={2: None, 3: None, 4: None, 5: 0},
        outside_outs=(0,),
    )
    (sums,) = call(add_kernel, [shape((regions, 1, 128), F32)], [sums])
    sums = lax.all_to_all(sums, "geo", split_axis=0, concat_axis=0, tiled=True)
    point_total = points * peers * regions
    scale = -step_weight * groups / (point_total * components)
    (total,) = call(functools.partial(final_kernel, scale), [shape((1, groups), F32)], [sums])
    return result, total.reshape(groups)


def solution(mesh):
    in_specs = (
        P("freq", None, None, "geo"),
        P(None, None, ("geo", "freq")),
        P(),
        P(None, ("geo", "freq")),
        P(),
        P(),
        P(),
        P(None, "geo"),
        P(("geo", "freq")),
    )
    out_specs = (P(None, ("geo", "freq")), P())
    return jax.shard_map(shards, mesh=mesh, in_specs=in_specs, out_specs=out_specs, check_vma=False)
```

```python
import functools
import math

import jax
import jax.numpy as jnp
from jax import lax
from jax.experimental import pallas as pl
from jax.experimental.pallas import tpu as pltpu
from jax.sharding import PartitionSpec as P

F32 = jnp.float32
BF16 = jnp.bfloat16
step_weight = 0.25
PAD = 40
MIB = 1 << 20
PARTS = 4
WHOLE = pl.BlockSpec(memory_space=pltpu.VMEM)
OUTSIDE = pl.BlockSpec(memory_space=pl.ANY)


def call(kernel, outs, args, scratch=(), flops=0, late=None, parted=(), outside_outs=(), limit=32):
    late = {} if late is None else late
    places = sorted(late)
    size = sum(a.size * a.dtype.itemsize for a in (*args, *outs))
    args = [
        pltpu.with_memory_space_constraint(a, pltpu.HBM) if i in late else a
        for i, a in enumerate(args)
    ]
    n = len(args) + len(outs) + len(scratch)

    def body(*refs):
        given, kept, buffers = list(refs[: len(args)]), refs[len(args) : n], refs[n:]
        copies, sources = {}, {}
        order = sorted(range(len(places)), key=lambda k: math.prod(buffers[k].shape))
        for k in order:
            i = places[k]
            source = given[i] if late[i] is None else given[i].at[late[i]]
            sources[i], given[i] = source, buffers[k]
            if i not in parted:
                copies[i] = pltpu.make_async_copy(source, buffers[k], buffers[-1].at[k, 0])
                copies[i].start()
        for part in range(PARTS):
            for k in order:
                i = places[k]
                if i in parted:
                    source = sources[i]
                    rows = blocks_of(source.shape[0], PARTS)[part]
                    copies[i, part] = pltpu.make_async_copy(
                        source.at[rows, :], buffers[k].at[rows, :], buffers[-1].at[k, part]
                    )
                    copies[i, part].start()
        if places:
            kernel(*given, *kept, wait=lambda *which: [copies[i].wait() for i in which])
        else:
            kernel(*given, *kept)

    buffers = [
        pltpu.VMEM(args[i].shape if late[i] is None else args[i].shape[1:], args[i].dtype)
        for i in places
    ]
    if places:
        buffers.append(pltpu.SemaphoreType.DMA((len(places), PARTS)))
    return pl.pallas_call(
        body,
        out_shape=outs,
        in_specs=[OUTSIDE if i in late else WHOLE for i in range(len(args))],
        out_specs=[OUTSIDE if i in outside_outs else WHOLE for i in range(len(outs))],
        scratch_shapes=[*scratch, *buffers],
        compiler_params=pltpu.CompilerParams(vmem_limit_bytes=limit * MIB),
        cost_estimate=pl.CostEstimate(flops=flops, bytes_accessed=size, transcendentals=0),
    )(*args)


def shape(dims, kind):
    return jax.ShapeDtypeStruct(dims, kind)


def edge_picks(width, lon):
    row = lax.broadcasted_iota(jnp.int32, (16, width), 0)
    lane = lax.broadcasted_iota(jnp.int32, (16, width), 1)
    picks = jnp.zeros((16, width), F32)
    for half in range(width // lon):
        picks = jnp.where((row == half) & (lane == half * lon), 1.0, picks)
        picks = jnp.where((row == 8 + half) & (lane == half * lon + lon - 1), 1.0, picks)
    return picks.astype(BF16)


def take_edges(values, picks):
    return lax.dot_general(picks, values, (((1,), (1,)), ((), ())), preferred_element_type=F32)


def put_edges(from_west, from_east, width, lon):
    both = jnp.concatenate([from_west.astype(F32), from_east.astype(F32)], axis=0).astype(BF16)
    return lax.dot_general(
        both, edge_picks(width, lon), (((0,), (0,)), ((), ())), preferred_element_type=F32
    )


def split_rates(lon_rate, lat_rate):
    lon_abs, lat_abs = jnp.abs(lon_rate), jnp.abs(lat_rate)
    east = jnp.where(lon_rate > 0, lon_abs, 0.0)
    north = jnp.where(lat_rate > 0, lat_abs, 0.0)
    return 1.0 - lon_abs - lat_abs, east, lon_abs - east, north, lat_abs - north


def regroup_kernel(
    field_ref, mask_ref, lon_ref, lat_ref, rows_ref, west_ref, east_ref, rates_ref, wait
):
    directions, lat, lon = field_ref.shape
    freqs = lon_ref.shape[0]
    rows = directions * lat
    height = rates_ref.shape[1]
    rows_ref[0:PAD, :] = jnp.zeros((PAD, lon), F32)
    rows_ref[PAD + rows :, :] = jnp.zeros((PAD, lon), F32)
    own = lax.broadcasted_iota(jnp.int32, (freqs, lon), 0) == lax.axis_index("freq")
    own = own.astype(F32)
    wait(2, 3)
    for at in range(0, height, directions):
        for slot, ref in enumerate((lon_ref, lat_ref)):
            rates_ref[slot, at : at + directions, :] = lax.dot_general(
                ref[...], own, (((0,), (0,)), ((), ())),
                precision=lax.Precision.HIGHEST, preferred_element_type=F32,
            )
    wait(0, 1)
    mask = mask_ref[...].astype(F32)
    for d in range(directions):
        rows_ref[pl.ds(PAD + d, lat, stride=directions), :] = field_ref[d].astype(F32) * mask
    edges = take_edges(rows_ref[PAD : PAD + rows, :].astype(BF16), edge_picks(lon, lon))
    west_ref[...] = edges[0:8].astype(BF16)
    east_ref[...] = edges[8:16].astype(BF16)


def interior_kernel(rows_ref, rates_ref, part_ref, rate_ref, *, directions):
    peers, height, lon = part_ref.shape
    center, east, west, north, south = split_rates(rates_ref[0], rates_ref[1])
    lane = lax.broadcasted_iota(jnp.int32, (height, lon), 1)
    rate_ref[...] = jnp.where(lane == 0, west, east)
    east = jnp.where(lane == lon - 1, 0.0, east)
    west = jnp.where(lane == 0, 0.0, west)
    for r in range(peers):
        at = PAD + r * height
        here = rows_ref[at : at + height, :]
        part_ref[r] = (
            center * here
            + east * pltpu.roll(here, lon - 1, 1)
            + west * pltpu.roll(here, 1, 1)
            + north * rows_ref[at + directions : at + directions + height, :]
            + south * rows_ref[at - directions : at - directions + height, :]
        )


def edges_kernel(part_ref, rate_ref, west_ref, east_ref, out_any, out_ref, sems):
    peers, height, lon = part_ref.shape
    groups = blocks_of(peers, 4)
    copies = []
    cols = put_edges(west_ref[...], east_ref[...], lon, lon)
    rate = rate_ref[...]
    for i, group in enumerate(groups):
        for r in range(group.start, group.stop):
            out_ref[r] = (part_ref[r] + rate * cols[r * height : (r + 1) * height]).astype(BF16)
        copies.append(pltpu.make_async_copy(out_ref.at[group], out_any.at[group], sems.at[i]))
        copies[-1].start()
    for copy in copies:
        copy.wait()


def spread_rates(courant_refs, turn_scr, rates_scr):
    freqs, directions = courant_refs[0].shape
    for slot, ref in enumerate(courant_refs):
        turn_scr[...] = jnp.zeros_like(turn_scr)
        turn_scr[0:freqs, 0:directions] = ref[...]
        turned = turn_scr[...].T
        for f in range(freqs):
            rates_scr[slot, f * directions : (f + 1) * directions, :] = jnp.broadcast_to(
                turned[0:directions, f : f + 1], (directions, rates_scr.shape[2])
            )


def spread_factor(kappa_ref, factor_scr):
    freqs, points = kappa_ref.shape
    directions = factor_scr.shape[0] // freqs
    for f in range(freqs):
        factor_scr[f * directions : (f + 1) * directions, :] = jnp.broadcast_to(
            kappa_ref[f : f + 1, :], (directions, points)
        )


def decay_of(factor, coeff):
    return 1.0 - step_weight * (factor * coeff)


def forward(state_ref, inter_ref, factor_scr, coeff, rows):
    forced = jnp.dot(inter_ref[rows, :], square_of(state_ref), preferred_element_type=F32)
    here = state_ref[rows, :].astype(F32)
    return here, decay_of(factor_scr[rows, :], coeff) * here + step_weight * forced


def square_of(state_ref):
    state = state_ref[...]
    return state * state


def blocks_of(size, count):
    return [slice(at, at + size // count) for at in range(0, size, size // count)]


def pull_kernel(
    trajectory_ref, inter_ref, kappa_ref, coeff_ref, sed_ref,
    point_coeff_ref, next_ref, pull_ref, factor_scr, product_scr, wait,
):
    traj_ref = trajectory_ref.at[0]
    components, points = traj_ref.shape
    groups = coeff_ref.shape[1]
    blocks = blocks_of(components, 4)
    wait(2, 3, 4)
    sediment = sed_ref[...]
    hits = (lax.broadcasted_iota(jnp.int32, (groups, points), 0) == sediment).astype(F32)
    coeff = jnp.dot(
        jnp.broadcast_to(coeff_ref[...], (8, groups)), hits,
        precision=lax.Precision.HIGHEST, preferred_element_type=F32,
    )[0:1]
    point_coeff_ref[...] = coeff
    spread_factor(kappa_ref, factor_scr)
    for rows in blocks:
        here, after = forward(traj_ref, inter_ref, factor_scr, coeff, rows)
        next_ref[rows, :] = after
        product_scr[rows, :] = (0.5 * factor_scr[rows, :] * here * after).astype(BF16)
    product = product_scr[...]
    for rows in blocks:
        pushed = jnp.dot(inter_ref[rows, :], product, preferred_element_type=F32)
        factor, here = factor_scr[rows, :], traj_ref[rows, :].astype(F32)
        pull = factor * (next_ref[rows, :] + decay_of(factor, coeff) * here) + pushed
        pull_ref[rows, :] = pull.astype(BF16)


def states_kernel(
    trajectory_ref, inter_ref, kappa_ref, coeff_ref, courant_lon_ref, courant_lat_ref,
    turned_ref, next_ref, rates_ref, factor_scr, turn_scr, wait,
):
    traj_ref = trajectory_ref.at[1]
    components = traj_ref.shape[0]
    wait(2, 4, 5)
    spread_factor(kappa_ref, factor_scr)
    spread_rates((courant_lon_ref, courant_lat_ref), turn_scr, rates_ref)
    coeff = coeff_ref[...]
    turned_ref[...] = inter_ref[...].T
    for rows in blocks_of(components, 4):
        next_ref[rows, :] = forward(traj_ref, inter_ref, factor_scr, coeff, rows)[1]


def two_substeps(carried, turned_ref, kappa_ref, prepare, ready, write, weigh):
    m_scr, r_scr, factor_scr, product_scr = carried
    components, points = m_scr.shape
    blocks = blocks_of(components, PARTS)
    weights = jnp.zeros((8, points), F32)
    moved = r_scr[...]
    for rows in blocks:
        product_scr[rows, :] = jnp.dot(turned_ref[rows, :], moved, preferred_element_type=F32)
    coeff = prepare()
    spread_factor(kappa_ref, factor_scr)
    for rows in blocks:
        after, state = ready(rows)
        factor, old = factor_scr[rows, :], m_scr[rows, :]
        new = decay_of(factor, coeff) * old + 0.5 * (after * product_scr[rows, :])
        if weigh:
            terms = factor * (old * after + new * state)
            weights = weights + terms.reshape(-1, 8, points).sum(axis=0)
        m_scr[rows, :] = new
        r_scr[rows, :] = new.astype(BF16)
    moved = r_scr[...]
    for rows in blocks:
        pulled = jnp.dot(turned_ref[rows, :], moved, preferred_element_type=F32)
        state = ready(rows)[1]
        new = decay_of(factor_scr[rows, :], coeff) * m_scr[rows, :] + 0.5 * (state * pulled)
        write(rows, new)
    return weights


def first_kernel(
    moved_ref, turned_ref, kappa_ref, coeff_ref, mask_ref, next_ref, traj_ref,
    low_ref, high_ref, edge_ref, weights_ref, *carried, wait,
):
    freqs, height, lon = moved_ref.shape
    points = 2 * lon
    directions = height // 2
    m_scr, r_scr = carried[:2]
    for f in range(freqs):
        block = moved_ref[f].astype(F32)
        rows = slice(f * directions, (f + 1) * directions)
        m_scr[rows, 0:lon] = block[0:directions]
        m_scr[rows, lon:points] = block[directions:height]
    r_scr[...] = m_scr[...].astype(BF16)

    def prepare():
        wait(2, 3)
        return coeff_ref[...]

    def masks():
        return mask_ref[pl.ds(2 * lax.axis_index("freq"), 2), :].astype(F32)

    unread = list(range(PARTS))

    def ready(rows):
        if unread:
            part = unread.pop(0)
            wait((5, part), (6, part))
        return next_ref[rows, :], traj_ref[rows, :].astype(F32)

    def write(rows, values):
        if rows.start == 0:
            wait(4)
        mask = masks()
        low = (values[:, 0:lon] * mask[0:1]).astype(BF16)
        high = (values[:, lon:points] * mask[1:2]).astype(BF16)
        low_ref[rows, :] = low
        high_ref[rows, :] = high

    weights_ref[...] = two_substeps(
        carried, turned_ref, kappa_ref, prepare, ready, write, True
    )
    picks = edge_picks(points, lon)
    edges = take_edges(low_ref[...], picks[:, 0:lon]) + take_edges(high_ref[...], picks[:, lon:points])
    edge_ref[...] = edges.astype(BF16)


def inner_kernel(
    low_ref, high_ref, courant_ref, part_ref, edge_rate_ref, north_rate_ref, south_rate_ref
):
    components, lon = low_ref.shape
    chunk = 144
    lane = lax.broadcasted_iota(jnp.int32, (chunk, lon), 1)
    for rows in blocks_of(components, components // chunk):
        low, high = low_ref[rows, :].astype(F32), high_ref[rows, :].astype(F32)
        center, east, west, north, south = split_rates(
            courant_ref[0, rows, :], courant_ref[1, rows, :]
        )
        edge_rate_ref[rows, :] = jnp.where(lane == 0, west, east)
        north_rate_ref[rows, :] = north
        south_rate_ref[rows, :] = south
        east = jnp.where(lane == lon - 1, 0.0, east)
        west = jnp.where(lane == 0, 0.0, west)
        for half, (here, rate, other) in enumerate(((low, north, high), (high, south, low))):
            part_ref[rows, half * lon : (half + 1) * lon] = (
                center * here
                + east * pltpu.roll(here, lon - 1, 1)
                + west * pltpu.roll(here, 1, 1)
                + rate * other
            )


def halo_kernel(
    part_ref, edge_rate_ref, north_rate_ref, south_rate_ref, north_ref, south_ref, west_ref, east_ref,
    pull_ref, own_ref, sed_ref, moved_ref, sums_ref, wait,
):
    components, lon = north_ref.shape
    cols = put_edges(west_ref[...].astype(F32)[8:16], east_ref[...].astype(F32)[0:8], 2 * lon, lon)
    weights = [own_ref[:, 0:lon], own_ref[:, lon : 2 * lon]]
    for rows in blocks_of(components, components // 144):
        edge_rate = edge_rate_ref[rows, :]
        below = south_rate_ref[rows, :] * south_ref[rows, :].astype(F32)
        above = north_rate_ref[rows, :] * north_ref[rows, :].astype(F32)
        for half, outer in enumerate((below, above)):
            lanes = slice(half * lon, (half + 1) * lon)
            value = (part_ref[rows, lanes] + outer + edge_rate * cols[rows, lanes]).astype(BF16)
            moved_ref[rows, lanes] = value
            terms = value.astype(F32) * pull_ref[rows, lanes].astype(F32)
            weights[half] = weights[half] + terms.reshape(-1, 8, lon).sum(axis=0)
    wait(10)
    groups, points = sums_ref.shape[2], 2 * lon
    hits = (lax.broadcasted_iota(jnp.int32, (groups, points), 0) == sed_ref[...]).astype(F32)
    sums = lax.dot_general(
        jnp.concatenate(weights, axis=1), hits, (((1,), (1,)), ((), ())),
        precision=lax.Precision.HIGHEST, preferred_element_type=F32,
    )
    sums_ref[...] = jnp.broadcast_to(sums.sum(axis=0, keepdims=True)[None], sums_ref.shape)


def last_kernel(
    moved_ref, turned_ref, kappa_ref, coeff_ref, next_ref, traj_ref, out_any, *carried, wait
):
    *carried, out_ref, sems = carried
    copies = []
    m_scr, r_scr = carried[:2]
    r_scr[...] = moved_ref[...]
    m_scr[...] = moved_ref[...].astype(F32)

    def prepare():
        wait(2, 3)
        return coeff_ref[...]

    unread = list(range(PARTS))

    def ready(rows):
        if unread:
            part = unread.pop(0)
            wait((4, part), (5, part))
        return next_ref[rows, :], traj_ref[rows, :].astype(F32)

    def write(rows, values):
        out_ref[rows, :] = values.astype(BF16)
        copies.append(
            pltpu.make_async_copy(out_ref.at[rows, :], out_any.at[rows, :], sems.at[len(copies)])
        )
        copies[-1].start()

    two_substeps(carried, turned_ref, kappa_ref, prepare, ready, write, False)
    for copy in copies:
        copy.wait()


def add_kernel(parts_ref, out_ref):
    out_ref[...] = jnp.broadcast_to(parts_ref[...].sum(axis=0)[None], out_ref.shape)


def final_kernel(scale, parts_ref, out_ref):
    out_ref[...] = parts_ref[...].sum(axis=0)[:, 0 : out_ref.shape[1]] * scale


def shards(
    adjoint_final, trajectory, interaction, friction_factor, friction_coeff,
    courant_lon, courant_lat, sea_mask, sediment,
):
    freq_local, directions, lat, lon = adjoint_final.shape
    steps, components, points = trajectory.shape
    groups = friction_coeff.shape[0]
    peers, regions = lax.axis_size("freq"), lax.axis_size("geo")
    rows = directions * lat
    height = rows // peers
    eastward = [(i, (i + 1) % regions) for i in range(regions)]
    westward = [(j, i) for i, j in eastward]
    northward = [(i, i + 1) for i in range(peers - 1)]
    southward = [(j, i) for i, j in northward]

    field = adjoint_final.reshape(directions, lat, lon)
    grouped, west, east, own_rates = call(
        regroup_kernel,
        [
            shape((rows + 2 * PAD, lon), F32),
            shape((8, rows), BF16),
            shape((8, rows), BF16),
            shape((2, height, lon), F32),
        ],
        [field, sea_mask, courant_lon, courant_lat],
        late={0: None, 1: None, 2: None, 3: None},
    )
    from_west = lax.ppermute(east, "geo", eastward)
    from_east = lax.ppermute(west, "geo", westward)
    part, rate = call(
        functools.partial(interior_kernel, directions=directions),
        [shape((peers, height, lon), F32), shape((height, lon), F32)],
        [grouped, own_rates],
    )
    (sent,) = call(
        edges_kernel,
        [shape((peers, height, lon), BF16)],
        [part, rate, from_west, from_east],
        [pltpu.VMEM((peers, height, lon), BF16), pltpu.SemaphoreType.DMA((4,))],
        outside_outs=(0,),
    )
    sent, point_factor = lax.optimization_barrier((sent, friction_factor))
    moved = lax.all_to_all(sent, "freq", split_axis=0, concat_axis=0, tiled=True)

    product = 2 * components * components * points
    full, half_full = (components, points), (components, lon)
    coeff, next0, pull = call(
        pull_kernel,
        [shape((1, points), F32), shape(full, F32), shape(full, BF16)],
        [
            trajectory, interaction, point_factor, friction_coeff.reshape(1, groups),
            sediment.reshape(1, points),
        ],
        [pltpu.VMEM(full, F32), pltpu.VMEM(full, BF16)],
        flops=2 * product,
        late={2: None, 3: None, 4: None},
    )
    turned, next1, rates = call(
        states_kernel,
        [
            shape((components, components), BF16),
            shape(full, F32),
            shape((2, components, lon), F32),
        ],
        [trajectory, interaction, point_factor, coeff, courant_lon, courant_lat],
        [pltpu.VMEM(full, F32), pltpu.VMEM((128, 128), F32)],
        flops=product,
        late={2: None, 4: None, 5: None},
    )
    carried = [pltpu.VMEM(full, kind) for kind in (F32, BF16, F32, F32)]
    low, high, edges, weights = call(
        first_kernel,
        [
            shape(half_full, BF16),
            shape(half_full, BF16),
            shape((16, components), BF16),
            shape((8, points), F32),
        ],
        [moved, turned, friction_factor, coeff, sea_mask, next1, trajectory],
        carried,
        flops=2 * product,
        late={2: None, 3: None, 4: None, 5: None, 6: 1},
        parted=(5, 6),
    )
    above = lax.ppermute(low, "freq", southward)
    below = lax.ppermute(high, "freq", northward)
    from_west = lax.ppermute(edges, "geo", eastward)
    from_east = lax.ppermute(edges, "geo", westward)
    inner = call(
        inner_kernel,
        [shape(full, F32), shape(half_full, F32), shape(half_full, F32), shape(half_full, F32)],
        [low, high, rates],
    )
    moved, sums = call(
        halo_kernel,
        [shape(full, BF16), shape((peers, 1, 128), F32)],
        [*inner, above, below, from_west, from_east, pull, weights, sediment.reshape(1, points)],
        late={10: None},
    )
    sums = lax.all_to_all(sums, "freq", split_axis=0, concat_axis=0, tiled=True)
    sums, moved = lax.optimization_barrier((sums, moved))
    (result,) = call(
        last_kernel,
        [shape(full, BF16)],
        [moved, turned, friction_factor, coeff, next0, trajectory],
        [*carried, pltpu.VMEM(full, BF16), pltpu.SemaphoreType.DMA((4,))],
        flops=2 * product,
        late={2: None, 3: None, 4: None, 5: 0},
        parted=(4, 5),
        outside_outs=(0,),
    )
    (sums,) = call(add_kernel, [shape((regions, 1, 128), F32)], [sums])
    sums = lax.all_to_all(sums, "geo", split_axis=0, concat_axis=0, tiled=True)
    point_total = points * peers * regions
    scale = -step_weight * groups / (point_total * components)
    (total,) = call(functools.partial(final_kernel, scale), [shape((1, groups), F32)], [sums])
    return result, total.reshape(groups)


def solution(mesh):
    in_specs = (
        P("freq", None, None, "geo"),
        P(None, None, ("geo", "freq")),
        P(),
        P(None, ("geo", "freq")),
        P(),
        P(),
        P(),
        P(None, "geo"),
        P(("geo", "freq")),
    )
    out_specs = (P(None, ("geo", "freq")), P())
    return jax.shard_map(shards, mesh=mesh, in_specs=in_specs, out_specs=out_specs, check_vma=False)
```
